256 devices in a mesh: inst: 32 (over y, z_lo, core), tp: 8 (over x, z_hi).
Axes of the slice: x: 4, y: 4, z: 8 (z_hi: 2, z_lo: 4; z = z_hi * 4 + z_lo), core: 2. Of those that a mesh axis runs over, the one named last changes fastest.
Arguments:
- queries: bfloat16 [256, 8192], P('inst', 'tp'), may hold values from -8 to 8
- key_cache: bfloat16 [256, 512, 1024], P('inst', None, 'tp'), may hold values from -6 to 6
- cache_of_values: bfloat16 [256, 512, 1024], P('inst', None, 'tp'), may hold values from -6 to 6
- fresh_key_rows: bfloat16 [256, 1024], P('inst', 'tp'), may hold values from -6 to 6
- fresh_value_rows: bfloat16 [256, 1024], P('inst', 'tp'), may hold values from -6 to 6
- lengths: int32 [32, 8], replicated, may hold values from 1 to 512, 2304 in all within a row
- migrate_ids: int32 [32, 1], replicated, may hold values from 0 to 7, as said below
- partner: int32 [32], replicated, may hold values from 0 to 31, as said below
- migrant_queries: bfloat16 [32, 8192], P('inst', 'tp'), may hold values from -8 to 8
- mover_key_rows: bfloat16 [32, 1024], P('inst', 'tp'), may hold values from -6 to 6
- mover_value_rows: bfloat16 [32, 1024], P('inst', 'tp'), may hold values from -6 to 6
- out_weight: bfloat16 [8192, 4096], P('tp'), may hold values from -0.0625 to 0.0625
Outputs:
- resident_out: bfloat16 [256, 4096], P('inst')
- migrant_out: bfloat16 [32, 4096], P('inst')
The draws below stay inside these ranges and needn't reach their ends.
Inputs may be any that keep to these rules, and one draw needn't show every extreme that they name: partner[partner[i]] == i and partner[i] != i; some instance a is matched with a + 16. `migrate_ids`: the 1 ids of one instance are distinct.
All inputs are finite; a program needn't handle non-finite values.
Results may differ from the reference program's by a relative error of at most 0.007.
Values may be sent and summed in bfloat16 or wider, within the bound.
A program may use at most 64 MiB of HBM per device.

```python
import math
import jax
import jax.numpy as jnp
import numpy as np

HQ = 64
KEY_VALUE_HEADS = 8
HEAD_DIMENSION = 128
DOUT = 4096
SEQ = 8
CACHE_LENGTH = 512
MIG = 1
QUERY_PER_KEY = 8
INSTS = 32
STAYER_ROWS = 256
MOVER_ROWS = 32


def draw_head_block(key, token_count):
    base_offset = jnp.clip(jax.random.normal(key, (token_count, KEY_VALUE_HEADS, QUERY_PER_KEY, HEAD_DIMENSION), dtype=jnp.float32), -6.0, 6.0)
    return base_offset.reshape(token_count, HQ * HEAD_DIMENSION)


def draw_queries(key, part):
    key = jax.random.fold_in(key, 1)
    return draw_head_block(key, STAYER_ROWS).astype(jnp.bfloat16)


def draw_migrant_queries(key, part):
    key = jax.random.fold_in(key, 2)
    return draw_head_block(key, MOVER_ROWS).astype(jnp.bfloat16)


def draw_key_cache(key, part):
    key = jax.random.fold_in(key, 3)
    cache_store = jnp.clip(jax.random.normal(key, (STAYER_ROWS, CACHE_LENGTH, KEY_VALUE_HEADS * HEAD_DIMENSION), dtype=jnp.float32), -6.0, 6.0)
    return cache_store.astype(jnp.bfloat16)


def draw_migrate_ids(key, part):
    key = jax.random.fold_in(key, 4)
    keys_all = jax.random.split(key, INSTS)
    return jax.vmap(lambda single: jax.random.permutation(single, SEQ)[:MIG])(keys_all).astype(jnp.int32)


def draw_partner(key, part):
    key = jax.random.fold_in(key, 6)
    half_count = INSTS // 2
    anchor = jax.random.randint(jax.random.fold_in(key, 11), (), 0, half_count).astype(jnp.int32)
    order = jax.random.permutation(key, INSTS).astype(jnp.int32)
    spots = jnp.arange(INSTS, dtype=jnp.int32)
    placed_last = (order == anchor) | (order == anchor + half_count)
    priority = jnp.where(placed_last, spots + INSTS, spots)
    order = order[jnp.argsort(priority, stable=True)]
    firsts = order[0::2]
    seconds = order[1::2]
    matched = jnp.zeros((INSTS,), jnp.int32)
    matched = matched.at[firsts].set(seconds)
    matched = matched.at[seconds].set(firsts)
    return matched


def block_levels(own_key, dims, cuts, low, high):
    def one(axis_at, shards_of):
        steps = jax.random.uniform(jax.random.fold_in(jax.random.fold_in(own_key, 6), axis_at), (shards_of,), jnp.float32, low / len(cuts), high / len(cuts))
        return jnp.repeat(jnp.exp(steps), dims[axis_at] // shards_of).reshape((-1,) + (1,) * (len(dims) - axis_at - 1))

    factor_of = one(*cuts[0])
    for cut in cuts[1:]:
        factor_of = factor_of * one(*cut)
    return factor_of


def profile(number_of, total, limit, lean):
    weights = [(1 << 20) // math.isqrt(rank ** lean) + 1 for rank in range(2, number_of + 1)]
    rest, counts = total - limit - (number_of - 1), [1] * (number_of - 1)
    while rest > 0:
        free = [i for i in range(number_of - 1) if counts[i] < limit]
        pool, budget = sum([weights[i] for i in free]), rest
        for i in free:
            extra = min(limit - counts[i], max(1, budget * weights[i] // pool), rest)
            counts[i] = counts[i] + extra
            rest = rest - extra
    return np.array([limit] + counts)


def uneven_parts(key, amount, total, most, slope):
    if amount == 2:
        one = jax.random.randint(key, (), max(1, total - most), min(most, total - 1) + 1)
        return jnp.stack([one, total - one])
    tallies = jnp.asarray(profile(amount, total, most, slope), jnp.int32)
    twos = (amount - 1) // 2
    source_of, receiver = tallies[1:1 + 2 * twos:2], tallies[2:2 + 2 * twos:2]
    margin = jnp.minimum(source_of - 1, most - receiver)
    shifted = jax.random.randint(jax.random.fold_in(key, 1), (twos,), 0, 1 << 20) % (margin + 1)
    tallies = tallies.at[1:1 + 2 * twos:2].set(source_of - shifted).at[2:2 + 2 * twos:2].set(receiver + shifted)
    return tallies[jax.random.permutation(jax.random.fold_in(key, 2), amount)]


def scatter_about(rng, extent, spread, reach, cuts=(), held_as=jnp.bfloat16):
    drawn = jax.random.normal(rng, extent, jnp.float32) * spread
    if len(cuts) > 0:
        drawn = block_levels(rng, extent, cuts, -0.22, 0.18) * drawn
    return jnp.clip(drawn, min=-reach, max=reach).astype(held_as)


def setup_inputs(seed: int = 0) -> dict:
    key_of = jax.random.split(jax.random.key(seed), 13)
    return {
        "queries": draw_queries(jax.random.fold_in(key_of[12], 71), 0),
        "key_cache": draw_key_cache(jax.random.fold_in(key_of[12], 71), 0),
        "cache_of_values": scatter_about(key_of[2], (STAYER_ROWS, CACHE_LENGTH, KEY_VALUE_HEADS * HEAD_DIMENSION), 1.0, 6.0, ((0, 32), (2, 8))),
        "fresh_key_rows": scatter_about(key_of[3], (STAYER_ROWS, KEY_VALUE_HEADS * HEAD_DIMENSION), 1.0, 6.0, ((0, 32), (1, 8))),
        "fresh_value_rows": scatter_about(key_of[4], (STAYER_ROWS, KEY_VALUE_HEADS * HEAD_DIMENSION), 1.0, 6.0, ((0, 32), (1, 8))),
        "lengths": jax.vmap(lambda own: uneven_parts(own, SEQ, SEQ * CACHE_LENGTH // 2 + CACHE_LENGTH // 2, CACHE_LENGTH, 2))(jax.random.split(key_of[5], INSTS)).reshape((INSTS, SEQ)).astype(jnp.int32),
        "migrate_ids": draw_migrate_ids(jax.random.fold_in(key_of[12], 71), 0),
        "partner": draw_partner(jax.random.fold_in(key_of[12], 71), 0),
        "migrant_queries": draw_migrant_queries(jax.random.fold_in(key_of[12], 71), 0),
        "mover_key_rows": scatter_about(key_of[9], (MOVER_ROWS, KEY_VALUE_HEADS * HEAD_DIMENSION), 1.0, 6.0, ((0, 32), (1, 8))),
        "mover_value_rows": scatter_about(key_of[10], (MOVER_ROWS, KEY_VALUE_HEADS * HEAD_DIMENSION), 1.0, 6.0, ((0, 32), (1, 8))),
        "out_weight": scatter_about(key_of[11], (HQ * HEAD_DIMENSION, DOUT), (HQ * HEAD_DIMENSION) ** -0.5, 0.0625, ((0, 8),)),
    }


def attend(query_rows, key_rows, value_rows, new_key, new_value, seq_lengths):
    token_count = query_rows.shape[0]
    kv_heads = key_rows.shape[2] // HEAD_DIMENSION
    group = query_rows.shape[1] // (kv_heads * HEAD_DIMENSION)
    scaling = HEAD_DIMENSION ** -0.5
    queries_f = query_rows.astype(jnp.float32).reshape(token_count, kv_heads, group, HEAD_DIMENSION)
    keys_f = key_rows.astype(jnp.float32).reshape(token_count, -1, kv_heads, HEAD_DIMENSION)
    values_f = value_rows.astype(jnp.float32).reshape(token_count, -1, kv_heads, HEAD_DIMENSION)
    scores = jnp.einsum("rkgd,rlkd->rkgl", queries_f, keys_f) * scaling
    own = jnp.einsum("rkgd,rkd->rkg", queries_f, new_key.astype(jnp.float32).reshape(token_count, kv_heads, HEAD_DIMENSION)) * scaling
    positions = jnp.arange(keys_f.shape[1], dtype=jnp.int32)
    visible = (positions[None, :] < seq_lengths[:, None])[:, None, None, :]
    scores = jnp.where(visible, scores, jnp.float32(-1e30))
    top = jnp.maximum(jnp.max(scores, axis=-1), own)
    weights = jnp.where(visible, jnp.exp(scores - top[..., None]), jnp.float32(0.0))
    own_weight = jnp.exp(own - top)
    total = jnp.sum(weights, axis=-1) + own_weight
    probs = (weights / total[..., None]).astype(jnp.bfloat16)
    own_prob = (own_weight / total).astype(jnp.bfloat16)
    mixed = jnp.einsum("rkgl,rlkd->rkgd", probs.astype(jnp.float32), values_f)
    mixed = mixed + own_prob.astype(jnp.float32)[..., None] * new_value.astype(jnp.float32).reshape(token_count, kv_heads, 1, HEAD_DIMENSION)
    return mixed.reshape(token_count, -1).astype(jnp.bfloat16)


def reference(queries, key_cache, cache_of_values, fresh_key_rows, fresh_value_rows, lengths, migrate_ids, partner, migrant_queries, mover_key_rows, mover_value_rows, out_weight):
    resident_heads = attend(queries, key_cache, cache_of_values, fresh_key_rows, fresh_value_rows, lengths.reshape(-1))
    resident_out = jnp.dot(resident_heads, out_weight, preferred_element_type=jnp.float32).astype(jnp.bfloat16)
    row_ids = (partner[:, None] * SEQ + migrate_ids[partner]).reshape(-1).astype(jnp.int32)
    slab_keys = key_cache[row_ids]
    slab_values = cache_of_values[row_ids]
    slab_lengths = lengths.reshape(-1)[row_ids]
    migrant_heads = attend(migrant_queries, slab_keys, slab_values, mover_key_rows, mover_value_rows, slab_lengths)
    migrant_out = jnp.dot(migrant_heads, out_weight, preferred_element_type=jnp.float32).astype(jnp.bfloat16)
    return resident_out, migrant_out
```

```python
import functools

import jax
import jax.numpy as jnp
from jax import lax
from jax.experimental import pallas as pl
from jax.experimental.pallas import tpu as pltpu
from jax.sharding import PartitionSpec as P

HEAD = 128
GROUP = 8
PACK = 16
MESH = pl.DeviceIdType.MESH
F32, BF16 = jnp.float32, jnp.bfloat16


def wait_all(ref, sem):
    pltpu.make_async_copy(ref, ref, sem).wait()


def attend(queries, keys, values, own_keys, own_values, sizes):
    slots = keys[0].shape[0]
    rows = len(queries)
    scaling = HEAD**-0.5
    positions = lax.broadcasted_iota(jnp.int32, (GROUP, slots), 1)
    scores = [
        lax.dot_general(q, k, (((1,), (1,)), ((), ())), preferred_element_type=F32) * scaling
        for q, k in zip(queries, keys)
    ]
    own = [
        jnp.sum(q.astype(F32) * k.astype(F32), axis=1, keepdims=True) * scaling
        for q, k in zip(queries, own_keys)
    ]
    visible = [positions < n for n in sizes]
    scores = [jnp.where(m, s, jnp.float32(-1e30)) for m, s in zip(visible, scores)]
    top = [jnp.maximum(jnp.max(s, axis=1, keepdims=True), o) for s, o in zip(scores, own)]
    weights = [jnp.where(visible[j], jnp.exp(scores[j] - top[j]), 0.0) for j in range(rows)]
    own_weight = [jnp.exp(o - t) for o, t in zip(own, top)]
    total = [jnp.sum(w, axis=1, keepdims=True) + o for w, o in zip(weights, own_weight)]
    probs = [(w / t).astype(BF16) for w, t in zip(weights, total)]
    own_prob = [(o / t).astype(BF16).astype(F32) for o, t in zip(own_weight, total)]
    mixed = [jnp.dot(p, v, preferred_element_type=F32) for p, v in zip(probs, values)]
    return [
        (m + o * v.astype(F32)).astype(BF16) for m, o, v in zip(mixed, own_prob, own_values)
    ]


def kernel(
    n_inst, n_tp,
    queries, key_cache, value_cache, fresh_keys, fresh_values, lengths, migrate_ids, partner,
    migrant_queries, mover_keys, mover_values, weight,
    resident_out, migrant_out,
    q_in, k_in, v_in, mq_in, mk_in, mv_in, k_all, v_all, w_all, len_s, ids_s, partner_s,
    heads_f, q_buf, h_buf, rs_send, rs_buf, ag_buf, ar_buf,
    small_sem, k_sem, v_sem, w_sem, send_sem, recv_sem,
):
    me, mt = lax.axis_index("inst"), lax.axis_index("tp")
    rows = q_in.shape[0]
    dout = w_all.shape[1]
    part = dout // n_tp
    chunk = dout // PACK

    def inst_peer(k):
        return {"inst": lax.rem(me + k, n_inst)}

    def tp_peer(k):
        return {"tp": lax.rem(mt + k, n_tp)}

    barrier = pltpu.get_barrier_semaphore()

    def greet_inst(k, carry):
        pl.semaphore_signal(barrier, inc=1, device_id=inst_peer(k), device_id_type=MESH)
        return carry

    def greet_tp(k, carry):
        pl.semaphore_signal(barrier, inc=1, device_id=tp_peer(k), device_id_type=MESH)
        return carry

    lax.fori_loop(1, n_tp, greet_tp, 0)
    lax.fori_loop(1, n_inst, greet_inst, 0)

    small = [
        pltpu.make_async_copy(src, dst, small_sem.at[n])
        for n, (src, dst) in enumerate(
            (
                (migrant_queries, mq_in), (mover_keys, mk_in), (mover_values, mv_in),
                (queries, q_in), (fresh_keys, k_in), (fresh_values, v_in),
                (lengths, len_s), (migrate_ids, ids_s), (partner, partner_s),
            )
        )
    ]
    for c in small:
        c.start()
    k_copy = pltpu.make_async_copy(key_cache, k_all, k_sem)
    v_copy = pltpu.make_async_copy(value_cache, v_all, v_sem)
    w_copy = pltpu.make_async_copy(weight, w_all, w_sem)
    k_copy.start()
    v_copy.start()
    w_copy.start()

    for c in small[:3]:
        c.wait()
    mq = mq_in[...].astype(F32)
    block = jnp.concatenate(
        [mq[:, h * HEAD : (h + 1) * HEAD] for h in range(GROUP)]
        + [mk_in[...].astype(F32), mv_in[...].astype(F32)]
        + [jnp.zeros((PACK - GROUP - 2, HEAD), F32)],
        axis=0,
    )
    q_buf[me] = block.astype(BF16)
    pl.semaphore_wait(barrier, n_inst + n_tp - 2)

    def send_inst(buf, n):
        def body(k, carry):
            pltpu.make_async_remote_copy(
                buf.at[me], buf.at[me], send_sem.at[n], recv_sem.at[n],
                device_id=inst_peer(k), device_id_type=MESH,
            ).start()
            return carry

        lax.fori_loop(1, n_inst, body, 0)

    send_inst(q_buf, 0)

    for c in small[3:]:
        c.wait()
    k_copy.wait()
    v_copy.wait()
    q32 = q_in[...].astype(F32)
    k32, v32 = k_in[...].astype(F32), v_in[...].astype(F32)
    for h in range(GROUP):
        heads_f[:, h, :] = q32[:, h * HEAD : (h + 1) * HEAD]
    resident = attend(
        [heads_f[j].astype(BF16) for j in range(rows)],
        [k_all[j] for j in range(rows)],
        [v_all[j] for j in range(rows)],
        [k32[j : j + 1] for j in range(rows)],
        [v32[j : j + 1] for j in range(rows)],
        [len_s[me, j] for j in range(rows)],
    )
    for j in range(rows):
        heads_f[j] = resident[j].astype(F32)
    lhs = jnp.concatenate([heads_f[:, h, :] for h in range(GROUP)], axis=1).astype(BF16)
    w_copy.wait()

    def project(u):
        columns = pl.ds(pl.multiple_of(u * part, part), part)
        p = jnp.dot(lhs, w_all[:, columns], preferred_element_type=F32)
        return jnp.concatenate([p[:, : part // 2], p[:, part // 2 :]], axis=0).astype(BF16)

    def scatter(k, carry):
        u = lax.rem(mt + k, n_tp)
        rs_send[u] = project(u)
        pltpu.make_async_remote_copy(
            rs_send.at[u], rs_buf.at[mt], send_sem.at[1], recv_sem.at[1],
            device_id={"tp": u}, device_id_type=MESH,
        ).start()
        return carry

    lax.fori_loop(1, n_tp, scatter, 0)
    rs_buf[mt] = project(mt)

    wait_all(q_buf.at[pl.ds(0, n_inst - 1)], recv_sem.at[0])
    wait_all(q_buf.at[pl.ds(0, n_inst - 1)], send_sem.at[0])
    other = partner_s[me]
    row = ids_s[me, 0]
    arrived = q_buf[other].astype(F32)
    (served,) = attend(
        [arrived[:GROUP].astype(BF16)],
        [k_all[row]],
        [v_all[row]],
        [arrived[GROUP : GROUP + 1]],
        [arrived[GROUP + 1 : GROUP + 2]],
        [len_s[me, row]],
    )
    h_buf[me] = jnp.concatenate([served.astype(F32), jnp.zeros((PACK - GROUP, HEAD), F32)], axis=0).astype(BF16)
    send_inst(h_buf, 2)

    wait_all(rs_buf.at[pl.ds(0, n_tp - 1)], recv_sem.at[1])
    wait_all(rs_buf.at[pl.ds(0, n_tp - 1)], send_sem.at[1])
    total = rs_buf[0].astype(F32)
    for u in range(1, n_tp):
        total = total + rs_buf[u].astype(F32)
    ag_buf[mt] = total.astype(BF16)

    def gather(k, carry):
        pltpu.make_async_remote_copy(
            ag_buf.at[mt], ag_buf.at[mt], send_sem.at[3], recv_sem.at[3],
            device_id=tp_peer(k), device_id_type=MESH,
        ).start()
        return carry

    lax.fori_loop(1, n_tp, gather, 0)

    wait_all(h_buf.at[pl.ds(0, n_inst - 1)], recv_sem.at[2])
    wait_all(h_buf.at[pl.ds(0, n_inst - 1)], send_sem.at[2])
    mine = h_buf[other].astype(F32)
    mine = jnp.concatenate([mine[h : h + 1] for h in range(GROUP)], axis=1)
    mine = jnp.broadcast_to(mine, (PACK, GROUP * HEAD)).astype(BF16)
    row_of = lax.broadcasted_iota(jnp.int32, (PACK, chunk), 0)
    packed = jnp.zeros((PACK, chunk), F32)
    for c in range(PACK):
        p = jnp.dot(mine, w_all[:, c * chunk : (c + 1) * chunk], preferred_element_type=F32)
        packed = jnp.where(row_of == c, p, packed)
    ar_buf[mt] = packed.astype(BF16)

    def spread(k, carry):
        pltpu.make_async_remote_copy(
            ar_buf.at[mt], ar_buf.at[mt], send_sem.at[4], recv_sem.at[4],
            device_id=tp_peer(k), device_id_type=MESH,
        ).start()
        return carry

    lax.fori_loop(1, n_tp, spread, 0)

    wait_all(ag_buf.at[pl.ds(0, n_tp - 1)], recv_sem.at[3])
    wait_all(ag_buf.at[pl.ds(0, n_tp - 1)], send_sem.at[3])
    for u in range(n_tp):
        block = ag_buf[u].astype(F32)
        wide = jnp.concatenate([block[:rows], block[rows:]], axis=1)
        resident_out[:, u * part : (u + 1) * part] = wide.astype(BF16)

    wait_all(ar_buf.at[pl.ds(0, n_tp - 1)], recv_sem.at[4])
    wait_all(ar_buf.at[pl.ds(0, n_tp - 1)], send_sem.at[4])
    total = ar_buf[0].astype(F32)
    for u in range(1, n_tp):
        total = total + ar_buf[u].astype(F32)
    migrant_out[...] = jnp.concatenate([total[c : c + 1] for c in range(PACK)], axis=1).astype(BF16)


def on_device(n_inst, n_tp, *args):
    queries, key_cache, weight = args[0], args[1], args[11]
    rows, slots, _ = key_cache.shape
    dout = weight.shape[1]
    part = dout // n_tp
    vmem = pltpu.VMEM
    dma = pltpu.SemaphoreType.DMA
    return pl.pallas_call(
        functools.partial(kernel, n_inst, n_tp),
        out_shape=(
            jax.ShapeDtypeStruct((rows, dout), BF16),
            jax.ShapeDtypeStruct((1, dout), BF16),
        ),
        in_specs=[pl.BlockSpec(memory_space=pl.ANY)] * 12,
        out_specs=[pl.BlockSpec(memory_space=vmem)] * 2,
        scratch_shapes=[
            vmem((rows, GROUP * HEAD), BF16),
            vmem((rows, HEAD), BF16),
            vmem((rows, HEAD), BF16),
            vmem((1, GROUP * HEAD), BF16),
            vmem((1, HEAD), BF16),
            vmem((1, HEAD), BF16),
            vmem((rows, slots, HEAD), BF16),
            vmem((rows, slots, HEAD), BF16),
            vmem(weight.shape, BF16),
            pltpu.SMEM(args[5].shape, jnp.int32),
            pltpu.SMEM(args[6].shape, jnp.int32),
            pltpu.SMEM(args[7].shape, jnp.int32),
            vmem((rows, GROUP, HEAD), F32),
            vmem((n_inst, PACK, HEAD), BF16),
            vmem((n_inst, PACK, HEAD), BF16),
            vmem((n_tp, PACK, part // 2), BF16),
            vmem((n_tp, PACK, part // 2), BF16),
            vmem((n_tp, PACK, part // 2), BF16),
            vmem((n_tp, PACK, dout // PACK), BF16),
            dma((9,)),
            dma,
            dma,
            dma,
            dma((5,)),
            dma((5,)),
        ],
        compiler_params=pltpu.CompilerParams(
            collective_id=0, has_side_effects=True, vmem_limit_bytes=48 * 1024 * 1024
        ),
    )(*args)


def solution(mesh):
    in_specs = (
        P("inst", "tp"),
        P("inst", None, "tp"),
        P("inst", None, "tp"),
        P("inst", "tp"),
        P("inst", "tp"),
        P(),
        P(),
        P(),
        P("inst", "tp"),
        P("inst", "tp"),
        P("inst", "tp"),
        P("tp", None),
    )
    out_specs = (P("inst", None), P("inst", None))
    return jax.shard_map(
        functools.partial(on_device, mesh.shape["inst"], mesh.shape["tp"]),
        mesh=mesh, in_specs=in_specs, out_specs=out_specs, check_vma=False,
    )
```

```python
import functools

import jax
import jax.numpy as jnp
from jax import lax
from jax.experimental import pallas as pl
from jax.experimental.pallas import tpu as pltpu
from jax.sharding import PartitionSpec as P

HEAD = 128
GROUP = 8
PACK = 16
MESH = pl.DeviceIdType.MESH
F32, BF16 = jnp.float32, jnp.bfloat16


def wait_all(ref, sem):
    pltpu.make_async_copy(ref, ref, sem).wait()


def attend(queries, keys, values, own_keys, own_values, sizes):
    slots = keys[0].shape[0]
    rows = len(queries)
    scaling = HEAD**-0.5
    positions = lax.broadcasted_iota(jnp.int32, (GROUP, slots), 1)
    scores = [
        lax.dot_general(q, k, (((1,), (1,)), ((), ())), preferred_element_type=F32) * scaling
        for q, k in zip(queries, keys)
    ]
    own = [
        jnp.sum(q.astype(F32) * k.astype(F32), axis=1, keepdims=True) * scaling
        for q, k in zip(queries, own_keys)
    ]
    visible = [positions < n for n in sizes]
    scores = [jnp.where(m, s, jnp.float32(-1e30)) for m, s in zip(visible, scores)]
    top = [jnp.maximum(jnp.max(s, axis=1, keepdims=True), o) for s, o in zip(scores, own)]
    weights = [jnp.where(visible[j], jnp.exp(scores[j] - top[j]), 0.0) for j in range(rows)]
    own_weight = [jnp.exp(o - t) for o, t in zip(own, top)]
    total = [jnp.sum(w, axis=1, keepdims=True) + o for w, o in zip(weights, own_weight)]
    probs = [(w / t).astype(BF16) for w, t in zip(weights, total)]
    own_prob = [(o / t).astype(BF16).astype(F32) for o, t in zip(own_weight, total)]
    mixed = [jnp.dot(p, v, preferred_element_type=F32) for p, v in zip(probs, values)]
    return [
        (m + o * v.astype(F32)).astype(BF16) for m, o, v in zip(mixed, own_prob, own_values)
    ]


def kernel(
    n_inst, n_tp,
    queries, key_cache, value_cache, fresh_keys, fresh_values, lengths, migrate_ids, partner,
    migrant_queries, mover_keys, mover_values, weight,
    resident_out, migrant_out,
    q_in, k_in, v_in, mq_in, mk_in, mv_in, k_all, v_all, w_all, len_s, ids_s, partner_s,
    heads_f, q_buf, kv_buf, h_buf, x_send, x_buf, z_buf, g_buf, a_buf, b_buf,
    small_sem, k_sem, v_sem, w_sem, send_sem, recv_sem,
):
    me, mt = lax.axis_index("inst"), lax.axis_index("tp")
    n_x = n_tp // 2
    tx, tz = mt // 2, lax.rem(mt, 2)
    rows = q_in.shape[0]
    dout = w_all.shape[1]
    part = dout // n_x
    chunk = dout // PACK

    def send(src, dst, n, device):
        pltpu.make_async_remote_copy(
            src, dst, send_sem.at[n], recv_sem.at[n], device_id=device, device_id_type=MESH
        ).start()

    barrier = pltpu.get_barrier_semaphore()

    def greet_inst(k, carry):
        device = {"inst": lax.rem(me + k, n_inst)}
        pl.semaphore_signal(barrier, inc=1, device_id=device, device_id_type=MESH)
        return carry

    def greet_tp(k, carry):
        device = {"tp": lax.rem(mt + k, n_tp)}
        pl.semaphore_signal(barrier, inc=1, device_id=device, device_id_type=MESH)
        return carry

    lax.fori_loop(1, n_inst, greet_inst, 0)
    lax.fori_loop(1, n_tp, greet_tp, 0)

    small = [
        pltpu.make_async_copy(src, dst, small_sem.at[n])
        for n, (src, dst) in enumerate(
            (
                (migrant_queries, mq_in), (mover_keys, mk_in), (mover_values, mv_in),
                (queries, q_in), (fresh_keys, k_in), (fresh_values, v_in),
                (lengths, len_s), (migrate_ids, ids_s), (partner, partner_s),
            )
        )
    ]
    for c in small:
        c.start()
    k_copy = pltpu.make_async_copy(key_cache, k_all, k_sem)
    v_copy = pltpu.make_async_copy(value_cache, v_all, v_sem)
    w_copy = pltpu.make_async_copy(weight, w_all, w_sem)
    k_copy.start()
    v_copy.start()
    w_copy.start()

    for c in small[:3]:
        c.wait()
    mq = mq_in[...].astype(F32)
    q_buf[me] = jnp.concatenate(
        [mq[:, h * HEAD : (h + 1) * HEAD] for h in range(GROUP)], axis=0
    ).astype(BF16)
    kv_buf[me] = jnp.concatenate([mk_in[...].astype(F32), mv_in[...].astype(F32)], axis=0)
    pl.semaphore_wait(barrier, n_inst + n_tp - 2)
    order = far_first(n_inst)
    for k in order:
        send(q_buf.at[me], q_buf.at[me], 0, {"inst": me ^ k})
    for k in order:
        send(kv_buf.at[me], kv_buf.at[me], 1, {"inst": me ^ k})

    for c in small[3:]:
        c.wait()
    k_copy.wait()
    v_copy.wait()
    q32 = q_in[...].astype(F32)
    k32, v32 = k_in[...].astype(F32), v_in[...].astype(F32)
    for h in range(GROUP):
        heads_f[:, h, :] = q32[:, h * HEAD : (h + 1) * HEAD]
    resident = attend(
        [heads_f[j].astype(BF16) for j in range(rows)],
        [k_all[j] for j in range(rows)],
        [v_all[j] for j in range(rows)],
        [k32[j : j + 1] for j in range(rows)],
        [v32[j : j + 1] for j in range(rows)],
        [len_s[j, me] for j in range(rows)],
    )
    for j in range(rows):
        heads_f[j] = resident[j].astype(F32)
    lhs = jnp.concatenate([heads_f[:, h, :] for h in range(GROUP)], axis=1).astype(BF16)
    w_copy.wait()

    def project(u):
        columns = pl.ds(pl.multiple_of(u * part, part), part)
        p = jnp.dot(lhs, w_all[:, columns], preferred_element_type=F32)
        return jnp.concatenate([p[:, : part // 2], p[:, part // 2 :]], axis=0).astype(BF16)

    for k in range(1, n_x):
        u = lax.rem(tx + k, n_x)
        x_send[k] = project(u)
        send(x_send.at[k], x_buf.at[tx], 2, {"tp": u * 2 + tz})
    x_buf[tx] = project(tx)

    wait_all(x_buf.at[pl.ds(0, n_x - 1)], recv_sem.at[2])
    total = x_buf[0].astype(F32)
    for u in range(1, n_x):
        total = total + x_buf[u].astype(F32)
    z_buf[0] = total.astype(BF16)
    send(z_buf.at[0], z_buf.at[1], 3, {"tp": mt + 1 - 2 * tz})

    other = partner_s[me]
    row = ids_s[0, me]
    wait_all(q_buf.at[pl.ds(0, n_inst - 1)], recv_sem.at[0])
    wait_all(kv_buf.at[pl.ds(0, n_inst - 1)], recv_sem.at[1])
    arrived = kv_buf[other]
    (served,) = attend(
        [q_buf[other]], [k_all[row]], [v_all[row]], [arrived[:1]], [arrived[1:]], [len_s[row, me]]
    )
    h_buf[me] = served
    for k in order:
        send(h_buf.at[me], h_buf.at[me], 4, {"inst": me ^ k})

    wait_all(z_buf.at[1], recv_sem.at[3])
    g_buf[tx] = (z_buf[0].astype(F32) + z_buf[1].astype(F32)).astype(BF16)
    for k in range(1, n_x):
        send(g_buf.at[tx], g_buf.at[tx], 5, {"tp": lax.rem(tx + k, n_x) * 2 + tz})

    wait_all(h_buf.at[pl.ds(0, n_inst - 1)], recv_sem.at[4])
    mine = h_buf[other].astype(F32)
    mine = jnp.concatenate([mine[h : h + 1] for h in range(GROUP)], axis=1)
    mine = jnp.broadcast_to(mine, (PACK, GROUP * HEAD)).astype(BF16)
    row_of = lax.broadcasted_iota(jnp.int32, (PACK, chunk // 2), 0)
    for n, buf in ((6, a_buf), (7, b_buf)):
        packed = jnp.zeros((PACK, chunk // 2), F32)
        for c in range(PACK // 2):
            first = (n - 6) * (dout // 2) + c * chunk
            p = jnp.dot(mine, w_all[:, first : first + chunk], preferred_element_type=F32)
            packed = jnp.where(row_of == 2 * c, p[:, : chunk // 2], packed)
            packed = jnp.where(row_of == 2 * c + 1, p[:, chunk // 2 :], packed)
        buf[mt] = packed.astype(BF16)
        for z in range(2):
            for k in reversed(range(n_x)):
                device = {"tp": lax.rem(tx + k, n_x) * 2 + z}
                if k == 0:
                    pl.when(tz != z)(lambda: send(buf.at[mt], buf.at[mt], n, device))
                else:
                    send(buf.at[mt], buf.at[mt], n, device)

    wait_all(g_buf.at[pl.ds(0, n_x - 1)], recv_sem.at[5])
    for u in range(n_x):
        block = g_buf[u].astype(F32)
        wide = jnp.concatenate([block[:rows], block[rows:]], axis=1)
        resident_out[:, u * part : (u + 1) * part] = wide.astype(BF16)

    for n, buf in ((6, a_buf), (7, b_buf)):
        wait_all(buf.at[pl.ds(0, n_tp - 1)], recv_sem.at[n])
        total = buf[0].astype(F32)
        for u in range(1, n_tp):
            total = total + buf[u].astype(F32)
        first = (n - 6) * (dout // 2)
        migrant_out[:, first : first + dout // 2] = jnp.concatenate(
            [total[c : c + 1] for c in range(PACK)], axis=1
        ).astype(BF16)

    wait_all(q_buf.at[pl.ds(0, n_inst - 1)], send_sem.at[0])
    wait_all(kv_buf.at[pl.ds(0, n_inst - 1)], send_sem.at[1])
    wait_all(x_buf.at[pl.ds(0, n_x - 1)], send_sem.at[2])
    wait_all(z_buf.at[1], send_sem.at[3])
    wait_all(h_buf.at[pl.ds(0, n_inst - 1)], send_sem.at[4])
    wait_all(g_buf.at[pl.ds(0, n_x - 1)], send_sem.at[5])
    wait_all(a_buf.at[pl.ds(0, n_tp - 1)], send_sem.at[6])
    wait_all(b_buf.at[pl.ds(0, n_tp - 1)], send_sem.at[7])


def far_first(n_inst):
    def hops(k):
        y, z = k // 8, k // 2 % 4
        return min(y, n_inst // 8 - y) + z

    return sorted(range(1, n_inst), key=lambda k: -hops(k))


def hand_over(resident, migrant, resident_out, migrant_out, sem):
    copies = [
        pltpu.make_async_copy(resident, resident_out, sem.at[0]),
        pltpu.make_async_copy(migrant, migrant_out, sem.at[1]),
    ]
    for c in copies:
        c.start()
    for c in copies:
        c.wait()


def on_device(n_inst, n_tp, *args):
    args = (*args[:5], args[5].T, args[6].T, *args[7:])
    key_cache, weight = args[1], args[11]
    rows, slots, _ = key_cache.shape
    dout = weight.shape[1]
    n_x = n_tp // 2
    block = (PACK, dout // n_x // 2)
    vmem = pltpu.VMEM
    dma = pltpu.SemaphoreType.DMA
    out_shape = (
        jax.ShapeDtypeStruct((rows, dout), BF16),
        jax.ShapeDtypeStruct((1, dout), BF16),
    )
    outs = pl.pallas_call(
        functools.partial(kernel, n_inst, n_tp),
        out_shape=out_shape,
        in_specs=[pl.BlockSpec(memory_space=pl.ANY)] * 12,
        out_specs=[pl.BlockSpec(memory_space=vmem)] * 2,
        scratch_shapes=[
            vmem((rows, GROUP * HEAD), BF16),
            vmem((rows, HEAD), BF16),
            vmem((rows, HEAD), BF16),
            vmem((1, GROUP * HEAD), BF16),
            vmem((1, HEAD), BF16),
            vmem((1, HEAD), BF16),
            vmem((rows, slots, HEAD), BF16),
            vmem((rows, slots, HEAD), BF16),
            vmem(weight.shape, BF16),
            pltpu.SMEM(args[5].shape, jnp.int32),
            pltpu.SMEM(args[6].shape, jnp.int32),
            pltpu.SMEM(args[7].shape, jnp.int32),
            vmem((rows, GROUP, HEAD), F32),
            vmem((n_inst, GROUP, HEAD), BF16),
            vmem((n_inst, 2, HEAD), F32),
            vmem((n_inst, GROUP, HEAD), BF16),
            vmem((n_x, *block), BF16),
            vmem((n_x, *block), BF16),
            vmem((2, *block), BF16),
            vmem((n_x, *block), BF16),
            vmem((n_tp, PACK, dout // PACK // 2), BF16),
            vmem((n_tp, PACK, dout // PACK // 2), BF16),
            dma((9,)),
            dma,
            dma,
            dma,
            dma((8,)),
            dma((8,)),
        ],
        compiler_params=pltpu.CompilerParams(
            collective_id=0, has_side_effects=True, vmem_limit_bytes=48 * 1024 * 1024
        ),
    )(*[pltpu.with_memory_space_constraint(a, pltpu.HBM) for a in args])
    return pl.pallas_call(
        hand_over,
        out_shape=out_shape,
        in_specs=[pl.BlockSpec(memory_space=vmem)] * 2,
        out_specs=[pl.BlockSpec(memory_space=pl.ANY)] * 2,
        scratch_shapes=[dma((2,))],
        compiler_params=pltpu.CompilerParams(vmem_limit_bytes=4 * 1024 * 1024),
    )(*outs)


def solution(mesh):
    in_specs = (
        P("inst", "tp"),
        P("inst", None, "tp"),
        P("inst", None, "tp"),
        P("inst", "tp"),
        P("inst", "tp"),
        P(),
        P(),
        P(),
        P("inst", "tp"),
        P("inst", "tp"),
        P("inst", "tp"),
        P("tp", None),
    )
    out_specs = (P("inst", None), P("inst", None))
    return jax.shard_map(
        functools.partial(on_device, mesh.shape["inst"], mesh.shape["tp"]),
        mesh=mesh, in_specs=in_specs, out_specs=out_specs, check_vma=False,
    )
```

```python
import functools

import jax
import jax.numpy as jnp
from jax import lax
from jax.experimental import pallas as pl
from jax.experimental.pallas import tpu as pltpu
from jax.sharding import PartitionSpec as P

HEAD = 128
GROUP = 8
PACK = 16
MESH = pl.DeviceIdType.MESH
F32, BF16 = jnp.float32, jnp.bfloat16


def wait_all(ref, sem):
    pltpu.make_async_copy(ref, ref, sem).wait()


def attend(queries, keys, values, own_keys, own_values, sizes):
    slots = keys[0].shape[0]
    rows = len(queries)
    scaling = HEAD**-0.5
    positions = lax.broadcasted_iota(jnp.int32, (GROUP, slots), 1)
    scores = [
        lax.dot_general(q, k, (((1,), (1,)), ((), ())), preferred_element_type=F32) * scaling
        for q, k in zip(queries, keys)
    ]
    own = [
        jnp.sum(q.astype(F32) * k.astype(F32), axis=1, keepdims=True) * scaling
        for q, k in zip(queries, own_keys)
    ]
    visible = [positions < n for n in sizes]
    scores = [jnp.where(m, s, jnp.float32(-1e30)) for m, s in zip(visible, scores)]
    top = [jnp.maximum(jnp.max(s, axis=1, keepdims=True), o) for s, o in zip(scores, own)]
    weights = [jnp.where(visible[j], jnp.exp(scores[j] - top[j]), 0.0) for j in range(rows)]
    own_weight = [jnp.exp(o - t) for o, t in zip(own, top)]
    total = [jnp.sum(w, axis=1, keepdims=True) + o for w, o in zip(weights, own_weight)]
    probs = [(w / t).astype(BF16) for w, t in zip(weights, total)]
    own_prob = [(o / t).astype(BF16).astype(F32) for o, t in zip(own_weight, total)]
    mixed = [jnp.dot(p, v, preferred_element_type=F32) for p, v in zip(probs, values)]
    return [
        (m + o * v.astype(F32)).astype(BF16) for m, o, v in zip(mixed, own_prob, own_values)
    ]


def kernel(
    n_inst, n_tp,
    queries, key_cache, value_cache, fresh_keys, fresh_values, lengths, migrate_ids, partner,
    migrant_queries, mover_keys, mover_values, weight,
    resident_out, migrant_out,
    q_in, k_in, v_in, mq_in, mk_in, mv_in, k_all, v_all, w_all, len_s, ids_s, partner_s,
    heads_f, q_buf, kv_buf, h_buf, x_send, x_buf, z_buf, g_buf, a_buf, b_buf,
    small_sem, k_sem, v_sem, w_sem, send_sem, recv_sem,
):
    me, mt = lax.axis_index("inst"), lax.axis_index("tp")
    n_x = n_tp // 2
    tx, tz = mt // 2, lax.rem(mt, 2)
    rows = q_in.shape[0]
    dout = w_all.shape[1]
    part = dout // n_x
    chunk = dout // PACK

    def send(src, dst, n, device):
        pltpu.make_async_remote_copy(
            src, dst, send_sem.at[n], recv_sem.at[n], device_id=device, device_id_type=MESH
        ).start()

    barrier = pltpu.get_barrier_semaphore()

    for k in (*range(1, n_tp, 2), *range(2, n_tp, 2)):
        device = {"tp": lax.rem(mt + k, n_tp)}
        pl.semaphore_signal(barrier, inc=1, device_id=device, device_id_type=MESH)
    order = far_first(n_inst)
    for k in order:
        pl.semaphore_signal(barrier, inc=1, device_id={"inst": me ^ k}, device_id_type=MESH)

    small = [
        pltpu.make_async_copy(src, dst, small_sem.at[n])
        for n, (src, dst) in enumerate(
            (
                (migrant_queries, mq_in), (mover_keys, mk_in), (mover_values, mv_in),
                (queries, q_in), (fresh_keys, k_in), (fresh_values, v_in),
                (lengths, len_s), (migrate_ids, ids_s), (partner, partner_s),
            )
        )
    ]
    for c in small:
        c.start()
    k_copy = pltpu.make_async_copy(key_cache, k_all, k_sem)
    v_copy = pltpu.make_async_copy(value_cache, v_all, v_sem)
    w_copy = pltpu.make_async_copy(weight, w_all, w_sem)
    k_copy.start()
    v_copy.start()
    w_copy.start()

    for c in small[:3]:
        c.wait()
    mq = mq_in[...].astype(F32)
    q_buf[me] = jnp.concatenate(
        [mq[:, h * HEAD : (h + 1) * HEAD] for h in range(GROUP)], axis=0
    ).astype(BF16)
    kv_buf[me] = jnp.concatenate([mk_in[...].astype(F32), mv_in[...].astype(F32)], axis=0).astype(BF16)
    pl.semaphore_wait(barrier, n_inst + n_tp - 2)
    for k in order:
        send(kv_buf.at[me], kv_buf.at[me], 1, {"inst": me ^ k})
        send(q_buf.at[me], q_buf.at[me], 0, {"inst": me ^ k})

    for c in small[3:]:
        c.wait()
    k_copy.wait()
    v_copy.wait()
    q32 = q_in[...].astype(F32)
    k32, v32 = k_in[...].astype(F32), v_in[...].astype(F32)
    for h in range(GROUP):
        heads_f[:, h, :] = q32[:, h * HEAD : (h + 1) * HEAD]
    resident = attend(
        [heads_f[j].astype(BF16) for j in range(rows)],
        [k_all[j] for j in range(rows)],
        [v_all[j] for j in range(rows)],
        [k32[j : j + 1] for j in range(rows)],
        [v32[j : j + 1] for j in range(rows)],
        [len_s[j, me] for j in range(rows)],
    )
    for j in range(rows):
        heads_f[j] = resident[j].astype(F32)
    lhs = jnp.concatenate([heads_f[:, h, :] for h in range(GROUP)], axis=1).astype(BF16)
    w_copy.wait()

    def project(u):
        columns = pl.ds(pl.multiple_of(u * part, part), part)
        p = jnp.dot(lhs, w_all[:, columns], preferred_element_type=F32)
        return jnp.concatenate([p[:, : part // 2], p[:, part // 2 :]], axis=0).astype(BF16)

    for k in range(1, n_x):
        u = lax.rem(tx + k, n_x)
        x_send[k] = project(u)
        send(x_send.at[k], x_buf.at[tx], 2, {"tp": u * 2 + tz})
    x_buf[tx] = project(tx)

    other = partner_s[me]
    row = ids_s[0, me]
    wait_all(q_buf.at[pl.ds(0, n_inst - 1)], recv_sem.at[0])
    wait_all(kv_buf.at[pl.ds(0, n_inst - 1)], recv_sem.at[1])
    arrived = kv_buf[other].astype(F32)
    (served,) = attend(
        [q_buf[other]], [k_all[row]], [v_all[row]], [arrived[:1]], [arrived[1:]], [len_s[row, me]]
    )
    h_buf[me] = served
    for k in order:
        send(h_buf.at[me], h_buf.at[me], 4, {"inst": me ^ k})

    wait_all(x_buf.at[pl.ds(0, n_x - 1)], recv_sem.at[2])
    total = x_buf[0].astype(F32)
    for u in range(1, n_x):
        total = total + x_buf[u].astype(F32)
    z_buf[0] = total.astype(BF16)
    send(z_buf.at[0], z_buf.at[1], 3, {"tp": mt + 1 - 2 * tz})

    wait_all(h_buf.at[pl.ds(0, n_inst - 1)], recv_sem.at[4])
    mine = h_buf[other].astype(F32)
    mine = jnp.concatenate([mine[h : h + 1] for h in range(GROUP)], axis=1)
    mine = jnp.broadcast_to(mine, (PACK, GROUP * HEAD)).astype(BF16)
    row_of = lax.broadcasted_iota(jnp.int32, (PACK, chunk // 2), 0)
    for n, buf in ((6, a_buf), (7, b_buf)):
        packed = jnp.zeros((PACK, chunk // 2), F32)
        for c in range(PACK // 2):
            first = (n - 6) * (dout // 2) + c * chunk
            p = jnp.dot(mine, w_all[:, first : first + chunk], preferred_element_type=F32)
            packed = jnp.where(row_of == 2 * c, p[:, : chunk // 2], packed)
            packed = jnp.where(row_of == 2 * c + 1, p[:, chunk // 2 :], packed)
        buf[mt] = packed.astype(BF16)
        for z in range(2):
            for k in reversed(range(n_x)):
                device = {"tp": lax.rem(tx + k, n_x) * 2 + z}
                if k == 0:
                    pl.when(tz != z)(lambda: send(buf.at[mt], buf.at[mt], n, device))
                else:
                    send(buf.at[mt], buf.at[mt], n, device)

    wait_all(z_buf.at[1], recv_sem.at[3])
    g_buf[tx] = (z_buf[0].astype(F32) + z_buf[1].astype(F32)).astype(BF16)
    for k in range(1, n_x):
        send(g_buf.at[tx], g_buf.at[tx], 5, {"tp": lax.rem(tx + k, n_x) * 2 + tz})

    wait_all(g_buf.at[pl.ds(0, n_x - 1)], recv_sem.at[5])
    for u in range(n_x):
        block = g_buf[u].astype(F32)
        wide = jnp.concatenate([block[:rows], block[rows:]], axis=1)
        resident_out[:, u * part : (u + 1) * part] = wide.astype(BF16)

    for n, buf in ((6, a_buf), (7, b_buf)):
        wait_all(buf.at[pl.ds(0, n_tp - 1)], recv_sem.at[n])
        total = buf[0].astype(F32)
        for u in range(1, n_tp):
            total = total + buf[u].astype(F32)
        first = (n - 6) * (dout // 2)
        migrant_out[:, first : first + dout // 2] = jnp.concatenate(
            [total[c : c + 1] for c in range(PACK)], axis=1
        ).astype(BF16)

    wait_all(q_buf.at[pl.ds(0, n_inst - 1)], send_sem.at[0])
    wait_all(kv_buf.at[pl.ds(0, n_inst - 1)], send_sem.at[1])
    wait_all(x_buf.at[pl.ds(0, n_x - 1)], send_sem.at[2])
    wait_all(z_buf.at[1], send_sem.at[3])
    wait_all(h_buf.at[pl.ds(0, n_inst - 1)], send_sem.at[4])
    wait_all(g_buf.at[pl.ds(0, n_x - 1)], send_sem.at[5])
    wait_all(a_buf.at[pl.ds(0, n_tp - 1)], send_sem.at[6])
    wait_all(b_buf.at[pl.ds(0, n_tp - 1)], send_sem.at[7])


def far_first(n_inst):
    def hops(k):
        y, z = k // 8, k // 2 % 4
        return min(y, n_inst // 8 - y) + z

    return sorted(range(1, n_inst), key=lambda k: -hops(k))


def hand_over(resident, migrant, resident_out, migrant_out, sem):
    copies = [
        pltpu.make_async_copy(resident, resident_out, sem.at[0]),
        pltpu.make_async_copy(migrant, migrant_out, sem.at[1]),
    ]
    for c in copies:
        c.start()
    for c in copies:
        c.wait()


def on_device(n_inst, n_tp, *args):
    args = (*args[:5], args[5].T, args[6].T, *args[7:])
    key_cache, weight = args[1], args[11]
    rows, slots, _ = key_cache.shape
    dout = weight.shape[1]
    n_x = n_tp // 2
    block = (PACK, dout // n_x // 2)
    vmem = pltpu.VMEM
    dma = pltpu.SemaphoreType.DMA
    out_shape = (
        jax.ShapeDtypeStruct((rows, dout), BF16),
        jax.ShapeDtypeStruct((1, dout), BF16),
    )
    outs = pl.pallas_call(
        functools.partial(kernel, n_inst, n_tp),
        out_shape=out_shape,
        in_specs=[pl.BlockSpec(memory_space=pl.ANY)] * 12,
        out_specs=[pl.BlockSpec(memory_space=vmem)] * 2,
        scratch_shapes=[
            vmem((rows, GROUP * HEAD), BF16),
            vmem((rows, HEAD), BF16),
            vmem((rows, HEAD), BF16),
            vmem((1, GROUP * HEAD), BF16),
            vmem((1, HEAD), BF16),
            vmem((1, HEAD), BF16),
            vmem((rows, slots, HEAD), BF16),
            vmem((rows, slots, HEAD), BF16),
            vmem(weight.shape, BF16),
            pltpu.SMEM(args[5].shape, jnp.int32),
            pltpu.SMEM(args[6].shape, jnp.int32),
            pltpu.SMEM(args[7].shape, jnp.int32),
            vmem((rows, GROUP, HEAD), F32),
            vmem((n_inst, GROUP, HEAD), BF16),
            vmem((n_inst, 2, HEAD), BF16),
            vmem((n_inst, GROUP, HEAD), BF16),
            vmem((n_x, *block), BF16),
            vmem((n_x, *block), BF16),
            vmem((2, *block), BF16),
            vmem((n_x, *block), BF16),
            vmem((n_tp, PACK, dout // PACK // 2), BF16),
            vmem((n_tp, PACK, dout // PACK // 2), BF16),
            dma((9,)),
            dma,
            dma,
            dma,
            dma((8,)),
            dma((8,)),
        ],
        compiler_params=pltpu.CompilerParams(
            collective_id=0, has_side_effects=True, vmem_limit_bytes=48 * 1024 * 1024
        ),
    )(*[pltpu.with_memory_space_constraint(a, pltpu.HBM) for a in args])
    return pl.pallas_call(
        hand_over,
        out_shape=out_shape,
        in_specs=[pl.BlockSpec(memory_space=vmem)] * 2,
        out_specs=[pl.BlockSpec(memory_space=pl.ANY)] * 2,
        scratch_shapes=[dma((2,))],
        compiler_params=pltpu.CompilerParams(vmem_limit_bytes=4 * 1024 * 1024),
    )(*outs)


def solution(mesh):
    in_specs = (
        P("inst", "tp"),
        P("inst", None, "tp"),
        P("inst", None, "tp"),
        P("inst", "tp"),
        P("inst", "tp"),
        P(),
        P(),
        P(),
        P("inst", "tp"),
        P("inst", "tp"),
        P("inst", "tp"),
        P("tp", None),
    )
    out_specs = (P("inst", None), P("inst", None))
    return jax.shard_map(
        functools.partial(on_device, mesh.shape["inst"], mesh.shape["tp"]),
        mesh=mesh, in_specs=in_specs, out_specs=out_specs, check_vma=False,
    )
```

```python
import functools

import jax
import jax.numpy as jnp
from jax import lax
from jax.experimental import pallas as pl
from jax.experimental.pallas import tpu as pltpu
from jax.sharding import PartitionSpec as P

HEAD = 128
GROUP = 8
PACK = 16
MESH = pl.DeviceIdType.MESH
F32, BF16 = jnp.float32, jnp.bfloat16


def wait_all(ref, sem):
    pltpu.make_async_copy(ref, ref, sem).wait()


def attend(queries, keys, values, own_keys, own_values, sizes):
    slots = keys[0].shape[0]
    rows = len(queries)
    scaling = HEAD**-0.5
    positions = lax.broadcasted_iota(jnp.int32, (GROUP, slots), 1)
    scores = [
        lax.dot_general(q, k, (((1,), (1,)), ((), ())), preferred_element_type=F32) * scaling
        for q, k in zip(queries, keys)
    ]
    own = [
        jnp.sum(q.astype(F32) * k.astype(F32), axis=1, keepdims=True) * scaling
        for q, k in zip(queries, own_keys)
    ]
    visible = [positions < n for n in sizes]
    scores = [jnp.where(m, s, jnp.float32(-1e30)) for m, s in zip(visible, scores)]
    top = [jnp.maximum(jnp.max(s, axis=1, keepdims=True), o) for s, o in zip(scores, own)]
    weights = [jnp.where(visible[j], jnp.exp(scores[j] - top[j]), 0.0) for j in range(rows)]
    own_weight = [jnp.exp(o - t) for o, t in zip(own, top)]
    total = [jnp.sum(w, axis=1, keepdims=True) + o for w, o in zip(weights, own_weight)]
    probs = [(w / t).astype(BF16) for w, t in zip(weights, total)]
    own_prob = [(o / t).astype(BF16).astype(F32) for o, t in zip(own_weight, total)]
    mixed = [jnp.dot(p, v, preferred_element_type=F32) for p, v in zip(probs, values)]
    return [
        (m + o * v.astype(F32)).astype(BF16) for m, o, v in zip(mixed, own_prob, own_values)
    ]


def kernel(
    n_inst, n_tp,
    queries, key_cache, value_cache, fresh_keys, fresh_values, lengths, migrate_ids, partner,
    migrant_queries, mover_keys, mover_values, weight,
    resident_out, migrant_out,
    q_in, k_in, v_in, mq_in, mk_in, mv_in, k_all, v_all, w_all, len_s, ids_s, partner_s,
    heads_f, q_buf, kv_buf, h_buf, x_send, x_buf, z_buf, g_buf, a_buf, b_buf,
    small_sem, k_sem, v_sem, w_sem, send_sem, recv_sem,
):
    me, mt = lax.axis_index("inst"), lax.axis_index("tp")
    n_x = n_tp // 2
    tx, tz = mt // 2, lax.rem(mt, 2)
    rows = q_in.shape[0]
    dout = w_all.shape[1]
    part = dout // n_x
    chunk = dout // PACK

    def send(src, dst, n, device):
        pltpu.make_async_remote_copy(
            src, dst, send_sem.at[n], recv_sem.at[n], device_id=device, device_id_type=MESH
        ).start()

    barrier = pltpu.get_barrier_semaphore()

    def served_by(inst, z):
        first = inst ^ (6 * z)
        return first, first ^ 2

    def greet(inst, tp):
        device = {"inst": inst, "tp": tp}
        pl.semaphore_signal(barrier, inc=1, device_id=device, device_id_type=MESH)

    for k in (*range(1, n_tp, 2), *range(2, n_tp, 2)):
        tp = lax.rem(mt + k, n_tp)
        for inst in served_by(me, lax.rem(tp, 2)):
            greet(inst, tp)

    @pl.when(tz == 0)
    def _():
        greet(me, mt + 1)

    @pl.when(tz == 1)
    def _():
        for k in range(1, n_x):
            greet(me, lax.rem(tx + k, n_x) * 2 + 1)

    order = far_first(n_inst)
    for k in order:
        pl.semaphore_signal(barrier, inc=1, device_id={"inst": me ^ k}, device_id_type=MESH)

    small = [
        pltpu.make_async_copy(src, dst, small_sem.at[n])
        for n, (src, dst) in enumerate(
            (
                (migrant_queries, mq_in), (mover_keys, mk_in), (mover_values, mv_in),
                (queries, q_in), (fresh_keys, k_in), (fresh_values, v_in),
                (lengths, len_s), (migrate_ids, ids_s), (partner, partner_s),
            )
        )
    ]
    for c in small:
        c.start()
    k_copy = pltpu.make_async_copy(key_cache, k_all, k_sem)
    v_copy = pltpu.make_async_copy(value_cache, v_all, v_sem)
    w_copy = pltpu.make_async_copy(weight, w_all, w_sem)
    k_copy.start()
    v_copy.start()
    w_copy.start()

    for c in small[:3]:
        c.wait()
    mq = mq_in[...].astype(F32)
    q_buf[me] = jnp.concatenate(
        [mq[:, h * HEAD : (h + 1) * HEAD] for h in range(GROUP)], axis=0
    ).astype(BF16)
    kv_buf[me] = jnp.concatenate([mk_in[...].astype(F32), mv_in[...].astype(F32)], axis=0).astype(BF16)
    pl.semaphore_wait(barrier, n_inst - 1 + 2 * (n_tp - 1) + n_x * tz)
    for k in order:
        send(kv_buf.at[me], kv_buf.at[me], 1, {"inst": me ^ k})
        send(q_buf.at[me], q_buf.at[me], 0, {"inst": me ^ k})

    for c in small[3:]:
        c.wait()
    k_copy.wait()
    v_copy.wait()
    q32 = q_in[...].astype(F32)
    k32, v32 = k_in[...].astype(F32), v_in[...].astype(F32)
    for h in range(GROUP):
        heads_f[:, h, :] = q32[:, h * HEAD : (h + 1) * HEAD]
    resident = attend(
        [heads_f[j].astype(BF16) for j in range(rows)],
        [k_all[j] for j in range(rows)],
        [v_all[j] for j in range(rows)],
        [k32[j : j + 1] for j in range(rows)],
        [v32[j : j + 1] for j in range(rows)],
        [len_s[j, me] for j in range(rows)],
    )
    for j in range(rows):
        heads_f[j] = resident[j].astype(F32)
    lhs = jnp.concatenate([heads_f[:, h, :] for h in range(GROUP)], axis=1).astype(BF16)
    w_copy.wait()

    def project(u):
        columns = pl.ds(pl.multiple_of(u * part, part), part)
        p = jnp.dot(lhs, w_all[:, columns], preferred_element_type=F32)
        return jnp.concatenate([p[:, : part // 2], p[:, part // 2 :]], axis=0).astype(BF16)

    for k in range(1, n_x):
        u = lax.rem(tx + k, n_x)
        x_send[k] = project(u)
        send(x_send.at[k], x_buf.at[tx], 2, {"tp": u * 2 + tz})
    x_buf[tx] = project(tx)

    other = partner_s[me]
    row = ids_s[0, me]
    wait_all(q_buf.at[pl.ds(0, n_inst - 1)], recv_sem.at[0])
    wait_all(kv_buf.at[pl.ds(0, n_inst - 1)], recv_sem.at[1])
    arrived = kv_buf[other].astype(F32)
    (served,) = attend(
        [q_buf[other]], [k_all[row]], [v_all[row]], [arrived[:1]], [arrived[1:]], [len_s[row, me]]
    )
    h_buf[me] = served
    for k in order:
        send(h_buf.at[me], h_buf.at[me], 4, {"inst": me ^ k})

    wait_all(x_buf.at[pl.ds(0, n_x - 1)], recv_sem.at[2])
    total = x_buf[0].astype(F32)
    for u in range(1, n_x):
        total = total + x_buf[u].astype(F32)
    z_buf[0] = total.astype(BF16)
    send(z_buf.at[0], z_buf.at[1], 3, {"tp": mt + 1 - 2 * tz})

    wait_all(h_buf.at[pl.ds(0, n_inst - 1)], recv_sem.at[4])
    half_of = lax.rem(me // 2, 2)
    pair = served_by(me, tz)
    heads = [h_buf[partner_s[inst]].astype(F32) for inst in pair]
    heads = [jnp.concatenate([m[h : h + 1] for h in range(GROUP)], axis=1) for m in heads]
    heads = jnp.concatenate(
        [jnp.broadcast_to(m, (PACK // 2, GROUP * HEAD)) for m in heads], axis=0
    ).astype(BF16)
    row_of = lax.rem(lax.broadcasted_iota(jnp.int32, (PACK, chunk), 0), PACK // 2)
    packed = jnp.zeros((PACK, chunk), F32)
    for c in range(PACK // 2):
        columns = pl.ds(pl.multiple_of(half_of * (dout // 2) + c * chunk, chunk), chunk)
        p = jnp.dot(heads, w_all[:, columns], preferred_element_type=F32)
        packed = jnp.where(row_of == c, p, packed)
    slot = half_of * n_tp + mt
    for n in range(2):
        b_buf[n] = packed[n * PACK // 2 : (n + 1) * PACK // 2].astype(BF16)

    @pl.when(tz == 0)
    def _():
        a_buf[slot] = b_buf[0]

    for z in range(2):
        for k in reversed(range(n_x)):
            tp = lax.rem(tx + k, n_x) * 2 + z
            for n in range(2):
                give = functools.partial(
                    send, b_buf.at[n], a_buf.at[slot], 6, {"inst": pair[n], "tp": tp}
                )
                if (z, k, n) == (0, 0, 0):
                    pl.when(tz == 1)(give)
                else:
                    give()

    wait_all(z_buf.at[1], recv_sem.at[3])
    g_buf[tx] = (z_buf[0].astype(F32) + z_buf[1].astype(F32)).astype(BF16)
    for k in range(1, n_x):
        send(g_buf.at[tx], g_buf.at[tx], 5, {"tp": lax.rem(tx + k, n_x) * 2 + tz})

    wait_all(g_buf.at[pl.ds(0, n_x - 1)], recv_sem.at[5])
    for u in range(n_x):
        block = g_buf[u].astype(F32)
        wide = jnp.concatenate([block[:rows], block[rows:]], axis=1)
        resident_out[:, u * part : (u + 1) * part] = wide.astype(BF16)

    def wait_sums(sem):
        pl.when(tz == 0)(lambda: wait_all(a_buf.at[pl.ds(0, 2 * n_tp - 1)], sem))
        pl.when(tz == 1)(lambda: wait_all(a_buf, sem))

    wait_sums(recv_sem.at[6])
    for half in range(2):
        total = a_buf[half * n_tp].astype(F32)
        for u in range(1, n_tp):
            total = total + a_buf[half * n_tp + u].astype(F32)
        first = half * (dout // 2)
        migrant_out[:, first : first + dout // 2] = jnp.concatenate(
            [total[c : c + 1] for c in range(PACK // 2)], axis=1
        ).astype(BF16)

    wait_all(q_buf.at[pl.ds(0, n_inst - 1)], send_sem.at[0])
    wait_all(kv_buf.at[pl.ds(0, n_inst - 1)], send_sem.at[1])
    wait_all(x_buf.at[pl.ds(0, n_x - 1)], send_sem.at[2])
    wait_all(z_buf.at[1], send_sem.at[3])
    wait_all(h_buf.at[pl.ds(0, n_inst - 1)], send_sem.at[4])
    wait_all(g_buf.at[pl.ds(0, n_x - 1)], send_sem.at[5])
    wait_sums(send_sem.at[6])


def far_first(n_inst):
    def hops(k):
        y, z = k // 8, k // 2 % 4
        return min(y, n_inst // 8 - y) + z

    return sorted(range(1, n_inst), key=lambda k: -hops(k))


def hand_over(resident, migrant, resident_out, migrant_out, sem):
    copies = [
        pltpu.make_async_copy(resident, resident_out, sem.at[0]),
        pltpu.make_async_copy(migrant, migrant_out, sem.at[1]),
    ]
    for c in copies:
        c.start()
    for c in copies:
        c.wait()


def on_device(n_inst, n_tp, *args):
    args = (*args[:5], args[5].T, args[6].T, *args[7:])
    key_cache, weight = args[1], args[11]
    rows, slots, _ = key_cache.shape
    dout = weight.shape[1]
    n_x = n_tp // 2
    block = (PACK, dout // n_x // 2)
    vmem = pltpu.VMEM
    dma = pltpu.SemaphoreType.DMA
    out_shape = (
        jax.ShapeDtypeStruct((rows, dout), BF16),
        jax.ShapeDtypeStruct((1, dout), BF16),
    )
    outs = pl.pallas_call(
        functools.partial(kernel, n_inst, n_tp),
        out_shape=out_shape,
        in_specs=[pl.BlockSpec(memory_space=pl.ANY)] * 12,
        out_specs=[pl.BlockSpec(memory_space=vmem)] * 2,
        scratch_shapes=[
            vmem((rows, GROUP * HEAD), BF16),
            vmem((rows, HEAD), BF16),
            vmem((rows, HEAD), BF16),
            vmem((1, GROUP * HEAD), BF16),
            vmem((1, HEAD), BF16),
            vmem((1, HEAD), BF16),
            vmem((rows, slots, HEAD), BF16),
            vmem((rows, slots, HEAD), BF16),
            vmem(weight.shape, BF16),
            pltpu.SMEM(args[5].shape, jnp.int32),
            pltpu.SMEM(args[6].shape, jnp.int32),
            pltpu.SMEM(args[7].shape, jnp.int32),
            vmem((rows, GROUP, HEAD), F32),
            vmem((n_inst, GROUP, HEAD), BF16),
            vmem((n_inst, 2, HEAD), BF16),
            vmem((n_inst, GROUP, HEAD), BF16),
            vmem((n_x, *block), BF16),
            vmem((n_x, *block), BF16),
            vmem((2, *block), BF16),
            vmem((n_x, *block), BF16),
            vmem((2 * n_tp, PACK // 2, dout // PACK), BF16),
            vmem((2, PACK // 2, dout // PACK), BF16),
            dma((9,)),
            dma,
            dma,
            dma,
            dma((7,)),
            dma((7,)),
        ],
        compiler_params=pltpu.CompilerParams(
            collective_id=0, has_side_effects=True, vmem_limit_bytes=48 * 1024 * 1024
        ),
    )(*[pltpu.with_memory_space_constraint(a, pltpu.HBM) for a in args])
    return pl.pallas_call(
        hand_over,
        out_shape=out_shape,
        in_specs=[pl.BlockSpec(memory_space=vmem)] * 2,
        out_specs=[pl.BlockSpec(memory_space=pl.ANY)] * 2,
        scratch_shapes=[dma((2,))],
        compiler_params=pltpu.CompilerParams(vmem_limit_bytes=4 * 1024 * 1024),
    )(*outs)


def solution(mesh):
    in_specs = (
        P("inst", "tp"),
        P("inst", None, "tp"),
        P("inst", None, "tp"),
        P("inst", "tp"),
        P("inst", "tp"),
        P(),
        P(),
        P(),
        P("inst", "tp"),
        P("inst", "tp"),
        P("inst", "tp"),
        P("tp", None),
    )
    out_specs = (P("inst", None), P("inst", None))
    return jax.shard_map(
        functools.partial(on_device, mesh.shape["inst"], mesh.shape["tp"]),
        mesh=mesh, in_specs=in_specs, out_specs=out_specs, check_vma=False,
    )
```

```python
import functools

import jax
import jax.numpy as jnp
from jax import lax
from jax.experimental import pallas as pl
from jax.experimental.pallas import tpu as pltpu
from jax.sharding import PartitionSpec as P

HEAD = 128
GROUP = 8
PACK = 16
MESH = pl.DeviceIdType.MESH
F32, BF16 = jnp.float32, jnp.bfloat16


def wait_all(ref, sem):
    pltpu.make_async_copy(ref, ref, sem).wait()


def attend(queries, keys, values, own_keys, own_values, sizes):
    slots = keys[0].shape[0]
    rows = len(queries)
    scaling = HEAD**-0.5
    positions = lax.broadcasted_iota(jnp.int32, (GROUP, slots), 1)
    scores = [
        lax.dot_general(q, k, (((1,), (1,)), ((), ())), preferred_element_type=F32) * scaling
        for q, k in zip(queries, keys)
    ]
    own = [
        jnp.sum(q.astype(F32) * k.astype(F32), axis=1, keepdims=True) * scaling
        for q, k in zip(queries, own_keys)
    ]
    visible = [positions < n for n in sizes]
    scores = [jnp.where(m, s, jnp.float32(-1e30)) for m, s in zip(visible, scores)]
    top = [jnp.maximum(jnp.max(s, axis=1, keepdims=True), o) for s, o in zip(scores, own)]
    weights = [jnp.where(visible[j], jnp.exp(scores[j] - top[j]), 0.0) for j in range(rows)]
    own_weight = [jnp.exp(o - t) for o, t in zip(own, top)]
    total = [jnp.sum(w, axis=1, keepdims=True) + o for w, o in zip(weights, own_weight)]
    probs = [(w / t).astype(BF16) for w, t in zip(weights, total)]
    own_prob = [(o / t).astype(BF16).astype(F32) for o, t in zip(own_weight, total)]
    mixed = [jnp.dot(p, v, preferred_element_type=F32) for p, v in zip(probs, values)]
    return [
        (m + o * v.astype(F32)).astype(BF16) for m, o, v in zip(mixed, own_prob, own_values)
    ]


def kernel(
    n_inst, n_tp,
    queries, key_cache, value_cache, fresh_keys, fresh_values, lengths, migrate_ids, partner,
    migrant_queries, mover_keys, mover_values, weight,
    resident_out, migrant_out,
    q_in, k_in, v_in, mq_in, mk_in, mv_in, k_all, v_all, w_all, len_s, ids_s, partner_s,
    heads_f, q_buf, kv_buf, h_buf, x_send, x_buf, z_buf, g_buf, a_buf, b_buf,
    small_sem, k_sem, v_sem, w_sem, send_sem, recv_sem,
):
    me, mt = lax.axis_index("inst"), lax.axis_index("tp")
    n_x = n_tp // 2
    tx, tz = mt // 2, lax.rem(mt, 2)
    rows = q_in.shape[0]
    dout = w_all.shape[1]
    part = dout // n_x
    chunk = dout // PACK

    def send(src, dst, n, device):
        pltpu.make_async_remote_copy(
            src, dst, send_sem.at[n], recv_sem.at[n], device_id=device, device_id_type=MESH
        ).start()

    barrier = pltpu.get_barrier_semaphore()

    def served_by(inst, z):
        first = inst ^ (6 * z)
        return first, first ^ 2

    def greet(inst, tp):
        device = {"inst": inst, "tp": tp}
        pl.semaphore_signal(barrier, inc=1, device_id=device, device_id_type=MESH)

    order = far_first(n_inst)
    for k in order:
        greet(me ^ k, mt)
    for k in (*range(1, n_tp, 2), *range(2, n_tp, 2)):
        tp = lax.rem(mt + k, n_tp)
        for inst in served_by(me, lax.rem(tp, 2)):
            greet(inst, tp)

    @pl.when(tz == 0)
    def _():
        greet(me, mt + 1)

    @pl.when(tz == 1)
    def _():
        for k in range(1, n_x):
            greet(me, lax.rem(tx + k, n_x) * 2 + 1)

    small = [
        pltpu.make_async_copy(src, dst, small_sem.at[n])
        for n, (src, dst) in enumerate(
            (
                (migrant_queries, mq_in), (mover_keys, mk_in), (mover_values, mv_in),
                (queries, q_in), (fresh_keys, k_in), (fresh_values, v_in),
                (lengths, len_s), (migrate_ids, ids_s), (partner, partner_s),
            )
        )
    ]
    for c in small:
        c.start()
    k_copy = pltpu.make_async_copy(key_cache, k_all, k_sem)
    v_copy = pltpu.make_async_copy(value_cache, v_all, v_sem)
    w_copy = pltpu.make_async_copy(weight, w_all, w_sem)
    k_copy.start()
    v_copy.start()
    w_copy.start()

    for c in small[:3]:
        c.wait()
    mq = mq_in[...].astype(F32)
    q_buf[me] = jnp.concatenate(
        [mq[:, h * HEAD : (h + 1) * HEAD] for h in range(GROUP)], axis=0
    ).astype(BF16)
    kv_buf[me] = jnp.concatenate([mk_in[...].astype(F32), mv_in[...].astype(F32)], axis=0).astype(BF16)
    pl.semaphore_wait(barrier, n_inst - 1 + 2 * (n_tp - 1) + n_x * tz)
    for k in order:
        send(kv_buf.at[me], kv_buf.at[me], 1, {"inst": me ^ k})
        send(q_buf.at[me], q_buf.at[me], 0, {"inst": me ^ k})

    for c in small[3:]:
        c.wait()
    k_copy.wait()
    v_copy.wait()
    q32 = q_in[...].astype(F32)
    k32, v32 = k_in[...].astype(F32), v_in[...].astype(F32)
    for h in range(GROUP):
        heads_f[:, h, :] = q32[:, h * HEAD : (h + 1) * HEAD]
    resident = attend(
        [heads_f[j].astype(BF16) for j in range(rows)],
        [k_all[j] for j in range(rows)],
        [v_all[j] for j in range(rows)],
        [k32[j : j + 1] for j in range(rows)],
        [v32[j : j + 1] for j in range(rows)],
        [len_s[j, me] for j in range(rows)],
    )
    for j in range(rows):
        heads_f[j] = resident[j].astype(F32)
    lhs = jnp.concatenate([heads_f[:, h, :] for h in range(GROUP)], axis=1).astype(BF16)
    w_copy.wait()

    def project(u):
        columns = pl.ds(pl.multiple_of(u * part, part), part)
        p = jnp.dot(lhs, w_all[:, columns], preferred_element_type=F32)
        return jnp.concatenate([p[:, : part // 2], p[:, part // 2 :]], axis=0).astype(BF16)

    for k in range(1, n_x):
        u = lax.rem(tx + k, n_x)
        x_send[k] = project(u)
        send(x_send.at[k], x_buf.at[tx], 2, {"tp": u * 2 + tz})
    x_buf[tx] = project(tx)

    other = partner_s[me]
    row = ids_s[0, me]
    wait_all(q_buf.at[pl.ds(0, n_inst - 1)], recv_sem.at[0])
    wait_all(kv_buf.at[pl.ds(0, n_inst - 1)], recv_sem.at[1])
    arrived = kv_buf[other].astype(F32)
    (served,) = attend(
        [q_buf[other]], [k_all[row]], [v_all[row]], [arrived[:1]], [arrived[1:]], [len_s[row, me]]
    )
    h_buf[me] = served
    for k in order:
        send(h_buf.at[me], h_buf.at[me], 4, {"inst": me ^ k})

    wait_all(x_buf.at[pl.ds(0, n_x - 1)], recv_sem.at[2])
    total = x_buf[0].astype(F32)
    for u in range(1, n_x):
        total = total + x_buf[u].astype(F32)
    z_buf[0] = total.astype(BF16)
    send(z_buf.at[0], z_buf.at[1], 3, {"tp": mt + 1 - 2 * tz})

    wait_all(h_buf.at[pl.ds(0, n_inst - 1)], recv_sem.at[4])
    half_of = lax.rem(me // 2, 2)
    pair = served_by(me, tz)
    heads = [h_buf[partner_s[inst]].astype(F32) for inst in pair]
    heads = [jnp.concatenate([m[h : h + 1] for h in range(GROUP)], axis=1) for m in heads]
    heads = jnp.concatenate(
        [jnp.broadcast_to(m, (PACK // 2, GROUP * HEAD)) for m in heads], axis=0
    ).astype(BF16)
    row_of = lax.rem(lax.broadcasted_iota(jnp.int32, (PACK, chunk), 0), PACK // 2)
    packed = jnp.zeros((PACK, chunk), F32)
    for c in range(PACK // 2):
        columns = pl.ds(pl.multiple_of(half_of * (dout // 2) + c * chunk, chunk), chunk)
        p = jnp.dot(heads, w_all[:, columns], preferred_element_type=F32)
        packed = jnp.where(row_of == c, p, packed)
    slot = half_of * n_tp + mt
    for n in range(2):
        b_buf[n] = packed[n * PACK // 2 : (n + 1) * PACK // 2].astype(BF16)

    @pl.when(tz == 0)
    def _():
        a_buf[slot] = b_buf[0]

    for z in range(2):
        for k in reversed(range(n_x)):
            tp = lax.rem(tx + k, n_x) * 2 + z
            for n in range(2):
                give = functools.partial(
                    send, b_buf.at[n], a_buf.at[slot], 6, {"inst": pair[n], "tp": tp}
                )
                if (z, k, n) == (0, 0, 0):
                    pl.when(tz == 1)(give)
                else:
                    give()

    wait_all(z_buf.at[1], recv_sem.at[3])
    g_buf[tx] = (z_buf[0].astype(F32) + z_buf[1].astype(F32)).astype(BF16)
    for k in range(1, n_x):
        send(g_buf.at[tx], g_buf.at[tx], 5, {"tp": lax.rem(tx + k, n_x) * 2 + tz})

    wait_all(g_buf.at[pl.ds(0, n_x - 1)], recv_sem.at[5])
    for u in range(n_x):
        block = g_buf[u].astype(F32)
        wide = jnp.concatenate([block[:rows], block[rows:]], axis=1)
        resident_out[:, u * part : (u + 1) * part] = wide.astype(BF16)

    def wait_sums(sem):
        pl.when(tz == 0)(lambda: wait_all(a_buf.at[pl.ds(0, 2 * n_tp - 1)], sem))
        pl.when(tz == 1)(lambda: wait_all(a_buf, sem))

    wait_sums(recv_sem.at[6])
    for half in range(2):
        total = a_buf[half * n_tp].astype(F32)
        for u in range(1, n_tp):
            total = total + a_buf[half * n_tp + u].astype(F32)
        first = half * (dout // 2)
        migrant_out[:, first : first + dout // 2] = jnp.concatenate(
            [total[c : c + 1] for c in range(PACK // 2)], axis=1
        ).astype(BF16)

    wait_all(q_buf.at[pl.ds(0, n_inst - 1)], send_sem.at[0])
    wait_all(kv_buf.at[pl.ds(0, n_inst - 1)], send_sem.at[1])
    wait_all(x_buf.at[pl.ds(0, n_x - 1)], send_sem.at[2])
    wait_all(z_buf.at[1], send_sem.at[3])
    wait_all(h_buf.at[pl.ds(0, n_inst - 1)], send_sem.at[4])
    wait_all(g_buf.at[pl.ds(0, n_x - 1)], send_sem.at[5])
    wait_sums(send_sem.at[6])


def far_first(n_inst):
    def hops(k):
        y, z = k // 8, k // 2 % 4
        return min(y, n_inst // 8 - y) + z

    return sorted(range(1, n_inst), key=lambda k: -hops(k))


def hand_over(resident, migrant, resident_out, migrant_out, sem):
    copies = [
        pltpu.make_async_copy(resident, resident_out, sem.at[0]),
        pltpu.make_async_copy(migrant, migrant_out, sem.at[1]),
    ]
    for c in copies:
        c.start()
    for c in copies:
        c.wait()


def on_device(n_inst, n_tp, *args):
    args = (*args[:5], args[5].T, args[6].T, *args[7:])
    key_cache, weight = args[1], args[11]
    rows, slots, _ = key_cache.shape
    dout = weight.shape[1]
    n_x = n_tp // 2
    block = (PACK, dout // n_x // 2)
    vmem = pltpu.VMEM
    dma = pltpu.SemaphoreType.DMA
    out_shape = (
        jax.ShapeDtypeStruct((rows, dout), BF16),
        jax.ShapeDtypeStruct((1, dout), BF16),
    )
    outs = pl.pallas_call(
        functools.partial(kernel, n_inst, n_tp),
        out_shape=out_shape,
        in_specs=[pl.BlockSpec(memory_space=pl.ANY)] * 12,
        out_specs=[pl.BlockSpec(memory_space=vmem)] * 2,
        scratch_shapes=[
            vmem((rows, GROUP * HEAD), BF16),
            vmem((rows, HEAD), BF16),
            vmem((rows, HEAD), BF16),
            vmem((1, GROUP * HEAD), BF16),
            vmem((1, HEAD), BF16),
            vmem((1, HEAD), BF16),
            vmem((rows, slots, HEAD), BF16),
            vmem((rows, slots, HEAD), BF16),
            vmem(weight.shape, BF16),
            pltpu.SMEM(args[5].shape, jnp.int32),
            pltpu.SMEM(args[6].shape, jnp.int32),
            pltpu.SMEM(args[7].shape, jnp.int32),
            vmem((rows, GROUP, HEAD), F32),
            vmem((n_inst, GROUP, HEAD), BF16),
            vmem((n_inst, 2, HEAD), BF16),
            vmem((n_inst, GROUP, HEAD), BF16),
            vmem((n_x, *block), BF16),
            vmem((n_x, *block), BF16),
            vmem((2, *block), BF16),
            vmem((n_x, *block), BF16),
            vmem((2 * n_tp, PACK // 2, dout // PACK), BF16),
            vmem((2, PACK // 2, dout // PACK), BF16),
            dma((9,)),
            dma,
            dma,
            dma,
            dma((7,)),
            dma((7,)),
        ],
        compiler_params=pltpu.CompilerParams(
            collective_id=0, has_side_effects=True, vmem_limit_bytes=48 * 1024 * 1024
        ),
    )(*[pltpu.with_memory_space_constraint(a, pltpu.HBM) for a in args])
    return pl.pallas_call(
        hand_over,
        out_shape=out_shape,
        in_specs=[pl.BlockSpec(memory_space=vmem)] * 2,
        out_specs=[pl.BlockSpec(memory_space=pl.ANY)] * 2,
        scratch_shapes=[dma((2,))],
        compiler_params=pltpu.CompilerParams(vmem_limit_bytes=4 * 1024 * 1024),
    )(*outs)


def solution(mesh):
    in_specs = (
        P("inst", "tp"),
        P("inst", None, "tp"),
        P("inst", None, "tp"),
        P("inst", "tp"),
        P("inst", "tp"),
        P(),
        P(),
        P(),
        P("inst", "tp"),
        P("inst", "tp"),
        P("inst", "tp"),
        P("tp", None),
    )
    out_specs = (P("inst", None), P("inst", None))
    return jax.shard_map(
        functools.partial(on_device, mesh.shape["inst"], mesh.shape["tp"]),
        mesh=mesh, in_specs=in_specs, out_specs=out_specs, check_vma=False,
    )
```

```python
import functools

import jax
import jax.numpy as jnp
from jax import lax
from jax.experimental import pallas as pl
from jax.experimental.pallas import tpu as pltpu
from jax.sharding import PartitionSpec as P

HEAD = 128
GROUP = 8
PACK = 16
MESH = pl.DeviceIdType.MESH
F32, BF16 = jnp.float32, jnp.bfloat16


def wait_all(ref, sem):
    pltpu.make_async_copy(ref, ref, sem).wait()


def attend(queries, keys, values, own_keys, own_values, sizes):
    slots = keys[0].shape[0]
    rows = len(queries)
    scaling = HEAD**-0.5
    positions = lax.broadcasted_iota(jnp.int32, (GROUP, slots), 1)
    scores = [
        lax.dot_general(q, k, (((1,), (1,)), ((), ())), preferred_element_type=F32) * scaling
        for q, k in zip(queries, keys)
    ]
    own = [
        jnp.sum(q.astype(F32) * k.astype(F32), axis=1, keepdims=True) * scaling
        for q, k in zip(queries, own_keys)
    ]
    visible = [positions < n for n in sizes]
    scores = [jnp.where(m, s, jnp.float32(-1e30)) for m, s in zip(visible, scores)]
    top = [jnp.maximum(jnp.max(s, axis=1, keepdims=True), o) for s, o in zip(scores, own)]
    weights = [jnp.where(visible[j], jnp.exp(scores[j] - top[j]), 0.0) for j in range(rows)]
    own_weight = [jnp.exp(o - t) for o, t in zip(own, top)]
    total = [jnp.sum(w, axis=1, keepdims=True) + o for w, o in zip(weights, own_weight)]
    probs = [(w / t).astype(BF16) for w, t in zip(weights, total)]
    own_prob = [(o / t).astype(BF16).astype(F32) for o, t in zip(own_weight, total)]
    mixed = [jnp.dot(p, v, preferred_element_type=F32) for p, v in zip(probs, values)]
    return [
        (m + o * v.astype(F32)).astype(BF16) for m, o, v in zip(mixed, own_prob, own_values)
    ]


def kernel(
    n_inst, n_tp,
    queries, key_cache, value_cache, fresh_keys, fresh_values, lengths, migrate_ids, partner,
    migrant_queries, mover_keys, mover_values, weight,
    resident_out, migrant_out,
    q_in, k_in, v_in, mq_in, mk_in, mv_in, k_all, v_all, w_all, len_s, ids_s, partner_s,
    heads_f, q_buf, kv_buf, h_buf, x_send, x_buf, z_buf, g_buf, a_buf, b_buf,
    small_sem, k_sem, v_sem, w_sem, send_sem, recv_sem,
):
    me, mt = lax.axis_index("inst"), lax.axis_index("tp")
    n_x = n_tp // 2
    tx, tz = mt // 2, lax.rem(mt, 2)
    rows = q_in.shape[0]
    dout = w_all.shape[1]
    part = dout // n_x
    chunk = dout // PACK

    def send(src, dst, n, device):
        pltpu.make_async_remote_copy(
            src, dst, send_sem.at[n], recv_sem.at[n], device_id=device, device_id_type=MESH
        ).start()

    barrier = pltpu.get_barrier_semaphore()

    def served_by(inst, z):
        first = inst ^ (6 * z)
        return first, first ^ 2

    def greet(inst, tp):
        device = {"inst": inst, "tp": tp}
        pl.semaphore_signal(barrier, inc=1, device_id=device, device_id_type=MESH)

    order = far_first(n_inst)
    for k in order:
        greet(me ^ k, mt)
    for k in (*range(1, n_tp, 2), *range(2, n_tp, 2)):
        tp = lax.rem(mt + k, n_tp)
        for inst in served_by(me, lax.rem(tp, 2)):
            greet(inst, tp)

    @pl.when(tz == 0)
    def _():
        greet(me, mt + 1)

    @pl.when(tz == 1)
    def _():
        for k in range(1, n_x):
            greet(me, lax.rem(tx + k, n_x) * 2 + 1)

    small = [
        pltpu.make_async_copy(src, dst, small_sem.at[n])
        for n, (src, dst) in enumerate(
            (
                (migrant_queries, mq_in), (mover_keys, mk_in), (mover_values, mv_in),
                (queries, q_in), (fresh_keys, k_in), (fresh_values, v_in),
                (lengths, len_s), (migrate_ids, ids_s), (partner, partner_s),
            )
        )
    ]
    for c in small:
        c.start()
    k_copy = pltpu.make_async_copy(key_cache, k_all, k_sem)
    v_copy = pltpu.make_async_copy(value_cache, v_all, v_sem)
    w_copy = pltpu.make_async_copy(weight, w_all, w_sem)
    k_copy.start()
    v_copy.start()
    w_copy.start()

    for c in small[:3]:
        c.wait()
    mq = mq_in[...].astype(F32)
    q_buf[me] = jnp.concatenate(
        [mq[:, h * HEAD : (h + 1) * HEAD] for h in range(GROUP)], axis=0
    ).astype(BF16)
    kv_buf[me] = jnp.concatenate([mk_in[...].astype(F32), mv_in[...].astype(F32)], axis=0).astype(BF16)
    pl.semaphore_wait(barrier, n_inst - 1 + 2 * (n_tp - 1) + n_x * tz)
    for k in order:
        send(kv_buf.at[me], kv_buf.at[me], 1, {"inst": me ^ k})
        send(q_buf.at[me], q_buf.at[me], 0, {"inst": me ^ k})

    for c in small[3:]:
        c.wait()
    k_copy.wait()
    v_copy.wait()
    q32 = q_in[...].astype(F32)
    k32, v32 = k_in[...].astype(F32), v_in[...].astype(F32)
    for h in range(GROUP):
        heads_f[:, h, :] = q32[:, h * HEAD : (h + 1) * HEAD]
    resident = attend(
        [heads_f[j].astype(BF16) for j in range(rows)],
        [k_all[j] for j in range(rows)],
        [v_all[j] for j in range(rows)],
        [k32[j : j + 1] for j in range(rows)],
        [v32[j : j + 1] for j in range(rows)],
        [len_s[j, me] for j in range(rows)],
    )
    for j in range(rows):
        heads_f[j] = resident[j].astype(F32)
    lhs = jnp.concatenate([heads_f[:, h, :] for h in range(GROUP)], axis=1).astype(BF16)
    w_copy.wait()

    def project(u):
        columns = pl.ds(pl.multiple_of(u * part, part), part)
        p = jnp.dot(lhs, w_all[:, columns], preferred_element_type=F32)
        return jnp.concatenate([p[:, : part // 2], p[:, part // 2 :]], axis=0).astype(BF16)

    for k in range(1, n_x):
        u = lax.rem(tx + k, n_x)
        x_send[k] = project(u)
        send(x_send.at[k], x_buf.at[tx], 2, {"tp": u * 2 + tz})
    x_buf[tx] = project(tx)

    other = partner_s[me]
    row = ids_s[0, me]
    wait_all(q_buf.at[pl.ds(0, n_inst - 1)], recv_sem.at[0])
    wait_all(kv_buf.at[pl.ds(0, n_inst - 1)], recv_sem.at[1])
    arrived = kv_buf[other].astype(F32)
    (served,) = attend(
        [q_buf[other]], [k_all[row]], [v_all[row]], [arrived[:1]], [arrived[1:]], [len_s[row, me]]
    )
    h_buf[me] = served
    for u in first_served(n_inst):
        pl.when(me != u)(lambda: send(h_buf.at[me], h_buf.at[me], 4, {"inst": u}))

    wait_all(x_buf.at[pl.ds(0, n_x - 1)], recv_sem.at[2])
    total = x_buf[0].astype(F32)
    for u in range(1, n_x):
        total = total + x_buf[u].astype(F32)
    z_buf[0] = total.astype(BF16)
    send(z_buf.at[0], z_buf.at[1], 3, {"tp": mt + 1 - 2 * tz})

    wait_all(h_buf.at[pl.ds(0, n_inst - 1)], recv_sem.at[4])
    half_of = lax.rem(me // 2, 2)
    pair = served_by(me, tz)
    heads = [h_buf[partner_s[inst]].astype(F32) for inst in pair]
    heads = [jnp.concatenate([m[h : h + 1] for h in range(GROUP)], axis=1) for m in heads]
    heads = jnp.concatenate(
        [jnp.broadcast_to(m, (PACK // 2, GROUP * HEAD)) for m in heads], axis=0
    ).astype(BF16)
    row_of = lax.rem(lax.broadcasted_iota(jnp.int32, (PACK, chunk), 0), PACK // 2)
    packed = jnp.zeros((PACK, chunk), F32)
    for c in range(PACK // 2):
        columns = pl.ds(pl.multiple_of(half_of * (dout // 2) + c * chunk, chunk), chunk)
        p = jnp.dot(heads, w_all[:, columns], preferred_element_type=F32)
        packed = jnp.where(row_of == c, p, packed)
    slot = half_of * n_tp + mt
    for n in range(2):
        b_buf[n] = packed[n * PACK // 2 : (n + 1) * PACK // 2].astype(BF16)

    @pl.when(tz == 0)
    def _():
        a_buf[slot] = b_buf[0]

    for z in range(2):
        for u in range(n_x):
            tp = u * 2 + z
            for n in range(2):
                give = functools.partial(
                    send, b_buf.at[n], a_buf.at[slot], 6, {"inst": pair[n], "tp": tp}
                )
                if z == 0 and n == 0:
                    pl.when(mt != tp)(give)
                else:
                    give()

    wait_all(z_buf.at[1], recv_sem.at[3])
    g_buf[tx] = (z_buf[0].astype(F32) + z_buf[1].astype(F32)).astype(BF16)
    for k in range(1, n_x):
        send(g_buf.at[tx], g_buf.at[tx], 5, {"tp": lax.rem(tx + k, n_x) * 2 + tz})

    wait_all(g_buf.at[pl.ds(0, n_x - 1)], recv_sem.at[5])
    for u in range(n_x):
        block = g_buf[u].astype(F32)
        wide = jnp.concatenate([block[:rows], block[rows:]], axis=1)
        resident_out[:, u * part : (u + 1) * part] = wide.astype(BF16)

    def wait_sums(sem):
        pl.when(tz == 0)(lambda: wait_all(a_buf.at[pl.ds(0, 2 * n_tp - 1)], sem))
        pl.when(tz == 1)(lambda: wait_all(a_buf, sem))

    wait_all(q_buf.at[pl.ds(0, n_inst - 1)], send_sem.at[0])
    wait_all(kv_buf.at[pl.ds(0, n_inst - 1)], send_sem.at[1])
    wait_all(x_buf.at[pl.ds(0, n_x - 1)], send_sem.at[2])
    wait_all(z_buf.at[1], send_sem.at[3])
    wait_all(h_buf.at[pl.ds(0, n_inst - 1)], send_sem.at[4])
    wait_all(g_buf.at[pl.ds(0, n_x - 1)], send_sem.at[5])
    wait_sums(recv_sem.at[6])
    for half in range(2):
        terms = [a_buf[half * n_tp + u].astype(F32) for u in range(n_tp)]
        while len(terms) > 1:
            terms = [a + b for a, b in zip(terms[::2], terms[1::2])]
        for c in range(PACK // 2):
            first = half * (dout // 2) + c * chunk
            migrant_out[:, first : first + chunk] = terms[0][c : c + 1].astype(BF16)

    wait_sums(send_sem.at[6])


def first_served(n_inst):
    head = [7, 5, 1, 3]
    return head + [u for u in range(n_inst) if u not in head]


def far_first(n_inst):
    def hops(k):
        y, z = k // 8, k // 2 % 4
        return min(y, n_inst // 8 - y) + z

    return sorted(range(1, n_inst), key=lambda k: -hops(k))


def hand_over(resident, migrant, resident_out, migrant_out, sem):
    copies = [
        pltpu.make_async_copy(resident, resident_out, sem.at[0]),
        pltpu.make_async_copy(migrant, migrant_out, sem.at[1]),
    ]
    for c in copies:
        c.start()
    for c in copies:
        c.wait()


def on_device(n_inst, n_tp, *args):
    args = (*args[:5], args[5].T, args[6].T, *args[7:])
    key_cache, weight = args[1], args[11]
    rows, slots, _ = key_cache.shape
    dout = weight.shape[1]
    n_x = n_tp // 2
    block = (PACK, dout // n_x // 2)
    vmem = pltpu.VMEM
    dma = pltpu.SemaphoreType.DMA
    out_shape = (
        jax.ShapeDtypeStruct((rows, dout), BF16),
        jax.ShapeDtypeStruct((1, dout), BF16),
    )
    outs = pl.pallas_call(
        functools.partial(kernel, n_inst, n_tp),
        out_shape=out_shape,
        in_specs=[pl.BlockSpec(memory_space=pl.ANY)] * 12,
        out_specs=[pl.BlockSpec(memory_space=vmem)] * 2,
        scratch_shapes=[
            vmem((rows, GROUP * HEAD), BF16),
            vmem((rows, HEAD), BF16),
            vmem((rows, HEAD), BF16),
            vmem((1, GROUP * HEAD), BF16),
            vmem((1, HEAD), BF16),
            vmem((1, HEAD), BF16),
            vmem((rows, slots, HEAD), BF16),
            vmem((rows, slots, HEAD), BF16),
            vmem(weight.shape, BF16),
            pltpu.SMEM(args[5].shape, jnp.int32),
            pltpu.SMEM(args[6].shape, jnp.int32),
            pltpu.SMEM(args[7].shape, jnp.int32),
            vmem((rows, GROUP, HEAD), F32),
            vmem((n_inst, GROUP, HEAD), BF16),
            vmem((n_inst, 2, HEAD), BF16),
            vmem((n_inst, GROUP, HEAD), BF16),
            vmem((n_x, *block), BF16),
            vmem((n_x, *block), BF16),
            vmem((2, *block), BF16),
            vmem((n_x, *block), BF16),
            vmem((2 * n_tp, PACK // 2, dout // PACK), BF16),
            vmem((2, PACK // 2, dout // PACK), BF16),
            dma((9,)),
            dma,
            dma,
            dma,
            dma((7,)),
            dma((7,)),
        ],
        compiler_params=pltpu.CompilerParams(
            collective_id=0, has_side_effects=True, vmem_limit_bytes=48 * 1024 * 1024
        ),
    )(*[pltpu.with_memory_space_constraint(a, pltpu.HBM) for a in args])
    return pl.pallas_call(
        hand_over,
        out_shape=out_shape,
        in_specs=[pl.BlockSpec(memory_space=vmem)] * 2,
        out_specs=[pl.BlockSpec(memory_space=pl.ANY)] * 2,
        scratch_shapes=[dma((2,))],
        compiler_params=pltpu.CompilerParams(vmem_limit_bytes=4 * 1024 * 1024),
    )(*outs)


def solution(mesh):
    in_specs = (
        P("inst", "tp"),
        P("inst", None, "tp"),
        P("inst", None, "tp"),
        P("inst", "tp"),
        P("inst", "tp"),
        P(),
        P(),
        P(),
        P("inst", "tp"),
        P("inst", "tp"),
        P("inst", "tp"),
        P("tp", None),
    )
    out_specs = (P("inst", None), P("inst", None))
    return jax.shard_map(
        functools.partial(on_device, mesh.shape["inst"], mesh.shape["tp"]),
        mesh=mesh, in_specs=in_specs, out_specs=out_specs, check_vma=False,
    )
```

```python
import functools

import jax
import jax.numpy as jnp
from jax import lax
from jax.experimental import pallas as pl
from jax.experimental.pallas import tpu as pltpu
from jax.sharding import PartitionSpec as P

HEAD = 128
GROUP = 8
PACK = 16
MESH = pl.DeviceIdType.MESH
F32, BF16 = jnp.float32, jnp.bfloat16


def wait_all(ref, sem):
    pltpu.make_async_copy(ref, ref, sem).wait()


def attend(queries, keys, values, own_keys, own_values, sizes):
    slots = keys[0].shape[0]
    rows = len(queries)
    scaling = HEAD**-0.5
    positions = lax.broadcasted_iota(jnp.int32, (GROUP, slots), 1)
    scores = [
        lax.dot_general(q, k, (((1,), (1,)), ((), ())), preferred_element_type=F32) * scaling
        for q, k in zip(queries, keys)
    ]
    own = [
        jnp.sum(q.astype(F32) * k.astype(F32), axis=1, keepdims=True) * scaling
        for q, k in zip(queries, own_keys)
    ]
    visible = [positions < n for n in sizes]
    scores = [jnp.where(m, s, jnp.float32(-1e30)) for m, s in zip(visible, scores)]
    top = [jnp.maximum(jnp.max(s, axis=1, keepdims=True), o) for s, o in zip(scores, own)]
    weights = [jnp.exp(scores[j] - top[j]) for j in range(rows)]
    own_weight = [jnp.exp(o - t) for o, t in zip(own, top)]
    total = [jnp.sum(w, axis=1, keepdims=True) + o for w, o in zip(weights, own_weight)]
    inverse = [1.0 / t for t in total]
    probs = [(w * r).astype(BF16) for w, r in zip(weights, inverse)]
    own_prob = [(o * r).astype(BF16).astype(F32) for o, r in zip(own_weight, inverse)]
    mixed = [jnp.dot(p, v, preferred_element_type=F32) for p, v in zip(probs, values)]
    return [
        (m + o * v.astype(F32)).astype(BF16) for m, o, v in zip(mixed, own_prob, own_values)
    ]


def kernel(
    n_inst, n_tp,
    queries, key_cache, value_cache, fresh_keys, fresh_values, lengths, migrate_ids, partner,
    migrant_queries, mover_keys, mover_values, weight,
    resident_out, migrant_out,
    q_in, k_in, v_in, mq_in, mk_in, mv_in, k_all, v_all, w_all, len_s, ids_s, partner_s,
    heads_f, q_buf, kv_buf, h_buf, x_send, x_buf, z_buf, g_buf, a_buf, b_buf,
    small_sem, k_sem, v_sem, w_sem, send_sem, recv_sem,
):
    me, mt = lax.axis_index("inst"), lax.axis_index("tp")
    n_x = n_tp // 2
    tx, tz = mt // 2, lax.rem(mt, 2)
    rows = q_in.shape[0]
    dout = w_all.shape[1]
    part = dout // n_x
    chunk = dout // PACK

    def send(src, dst, n, device):
        pltpu.make_async_remote_copy(
            src, dst, send_sem.at[n], recv_sem.at[n], device_id=device, device_id_type=MESH
        ).start()

    barrier = pltpu.get_barrier_semaphore()

    def served_by(inst, z):
        first = inst ^ (6 * z)
        return first, first ^ 2

    def greet(inst, tp):
        device = {"inst": inst, "tp": tp}
        pl.semaphore_signal(barrier, inc=1, device_id=device, device_id_type=MESH)

    order = far_first(n_inst)
    for k in order:
        greet(me ^ k, mt)
    for k in (*range(1, n_tp, 2), *range(2, n_tp, 2)):
        tp = lax.rem(mt + k, n_tp)
        for inst in served_by(me, lax.rem(tp, 2)):
            greet(inst, tp)

    @pl.when(tz == 0)
    def _():
        greet(me, mt + 1)

    @pl.when(tz == 1)
    def _():
        for k in range(1, n_x):
            greet(me, lax.rem(tx + k, n_x) * 2 + 1)

    small = [
        pltpu.make_async_copy(src, dst, small_sem.at[n])
        for n, (src, dst) in enumerate(
            (
                (migrant_queries, mq_in), (mover_keys, mk_in), (mover_values, mv_in),
                (queries, q_in), (fresh_keys, k_in), (fresh_values, v_in),
                (lengths, len_s), (migrate_ids, ids_s), (partner, partner_s),
            )
        )
    ]
    for c in small:
        c.start()
    k_copy = pltpu.make_async_copy(key_cache, k_all, k_sem)
    v_copy = pltpu.make_async_copy(value_cache, v_all, v_sem)
    w_copy = pltpu.make_async_copy(weight, w_all, w_sem)
    k_copy.start()
    v_copy.start()
    w_copy.start()

    for c in small[:3]:
        c.wait()
    mq = mq_in[...].astype(F32)
    q_buf[me] = jnp.concatenate(
        [mq[:, h * HEAD : (h + 1) * HEAD] for h in range(GROUP)], axis=0
    ).astype(BF16)
    kv_buf[me] = jnp.concatenate([mk_in[...].astype(F32), mv_in[...].astype(F32)], axis=0).astype(BF16)
    pl.semaphore_wait(barrier, n_inst - 1 + 2 * (n_tp - 1) + n_x * tz)
    for k in order:
        send(kv_buf.at[me], kv_buf.at[me], 1, {"inst": me ^ k})
        send(q_buf.at[me], q_buf.at[me], 0, {"inst": me ^ k})

    for c in small[3:]:
        c.wait()
    k_copy.wait()
    v_copy.wait()
    q32 = q_in[...].astype(F32)
    k32, v32 = k_in[...].astype(F32), v_in[...].astype(F32)
    for h in range(GROUP):
        heads_f[:, h, :] = q32[:, h * HEAD : (h + 1) * HEAD]
    resident = attend(
        [heads_f[j].astype(BF16) for j in range(rows)],
        [k_all[j] for j in range(rows)],
        [v_all[j] for j in range(rows)],
        [k32[j : j + 1] for j in range(rows)],
        [v32[j : j + 1] for j in range(rows)],
        [len_s[j, me] for j in range(rows)],
    )
    for j in range(rows):
        heads_f[j] = resident[j].astype(F32)
    lhs = jnp.concatenate([heads_f[:, h, :] for h in range(GROUP)], axis=1).astype(BF16)
    w_copy.wait()

    def project(u):
        columns = pl.ds(pl.multiple_of(u * part, part), part)
        p = jnp.dot(lhs, w_all[:, columns], preferred_element_type=F32)
        return jnp.concatenate([p[:, : part // 2], p[:, part // 2 :]], axis=0).astype(BF16)

    for k in range(1, n_x):
        u = lax.rem(tx + k, n_x)
        x_send[k] = project(u)
        send(x_send.at[k], x_buf.at[tx], 2, {"tp": u * 2 + tz})
    x_buf[tx] = project(tx)

    other = partner_s[me]
    row = ids_s[0, me]
    wait_all(q_buf.at[pl.ds(0, n_inst - 1)], recv_sem.at[0])
    wait_all(kv_buf.at[pl.ds(0, n_inst - 1)], recv_sem.at[1])
    arrived = kv_buf[other].astype(F32)
    (served,) = attend(
        [q_buf[other]], [k_all[row]], [v_all[row]], [arrived[:1]], [arrived[1:]], [len_s[row, me]]
    )
    h_buf[me] = served
    for u in first_served(n_inst):
        pl.when(me != u)(lambda: send(h_buf.at[me], h_buf.at[me], 4, {"inst": u}))

    wait_all(x_buf.at[pl.ds(0, n_x - 1)], recv_sem.at[2])
    total = x_buf[0].astype(F32)
    for u in range(1, n_x):
        total = total + x_buf[u].astype(F32)
    z_buf[0] = total.astype(BF16)
    send(z_buf.at[0], z_buf.at[1], 3, {"tp": mt + 1 - 2 * tz})

    wait_all(h_buf.at[pl.ds(0, n_inst - 1)], recv_sem.at[4])
    half_of = lax.rem(me // 2, 2)
    pair = served_by(me, tz)
    heads = [h_buf[partner_s[inst]].astype(F32) for inst in pair]
    heads = [jnp.concatenate([m[h : h + 1] for h in range(GROUP)], axis=1) for m in heads]
    heads = jnp.concatenate(
        [jnp.broadcast_to(m, (PACK // 2, GROUP * HEAD)) for m in heads], axis=0
    ).astype(BF16)
    row_of = lax.rem(lax.broadcasted_iota(jnp.int32, (PACK, chunk), 0), PACK // 2)
    packed = jnp.zeros((PACK, chunk), F32)
    for c in range(PACK // 2):
        columns = pl.ds(pl.multiple_of(half_of * (dout // 2) + c * chunk, chunk), chunk)
        p = jnp.dot(heads, w_all[:, columns], preferred_element_type=F32)
        packed = jnp.where(row_of == c, p, packed)
    slot = half_of * n_tp + mt
    for n in range(2):
        b_buf[n] = packed[n * PACK // 2 : (n + 1) * PACK // 2].astype(BF16)

    @pl.when(tz == 0)
    def _():
        a_buf[slot] = b_buf[0]

    for z in range(2):
        for u in range(n_x):
            tp = u * 2 + z
            for n in range(2):
                give = functools.partial(
                    send, b_buf.at[n], a_buf.at[slot], 6, {"inst": pair[n], "tp": tp}
                )
                if z == 0 and n == 0:
                    pl.when(mt != tp)(give)
                else:
                    give()

    wait_all(z_buf.at[1], recv_sem.at[3])
    g_buf[tx] = (z_buf[0].astype(F32) + z_buf[1].astype(F32)).astype(BF16)
    for k in range(1, n_x):
        send(g_buf.at[tx], g_buf.at[tx], 5, {"tp": lax.rem(tx + k, n_x) * 2 + tz})

    wait_all(g_buf.at[pl.ds(0, n_x - 1)], recv_sem.at[5])
    for u in range(n_x):
        block = g_buf[u].astype(F32)
        wide = jnp.concatenate([block[:rows], block[rows:]], axis=1)
        resident_out[:, u * part : (u + 1) * part] = wide.astype(BF16)

    def wait_sums(sem):
        pl.when(tz == 0)(lambda: wait_all(a_buf.at[pl.ds(0, 2 * n_tp - 1)], sem))
        pl.when(tz == 1)(lambda: wait_all(a_buf, sem))

    wait_all(q_buf.at[pl.ds(0, n_inst - 1)], send_sem.at[0])
    wait_all(kv_buf.at[pl.ds(0, n_inst - 1)], send_sem.at[1])
    wait_all(x_buf.at[pl.ds(0, n_x - 1)], send_sem.at[2])
    wait_all(z_buf.at[1], send_sem.at[3])
    wait_all(h_buf.at[pl.ds(0, n_inst - 1)], send_sem.at[4])
    wait_all(g_buf.at[pl.ds(0, n_x - 1)], send_sem.at[5])
    wait_sums(recv_sem.at[6])
    for half in range(2):
        terms = [a_buf[half * n_tp + u].astype(F32) for u in range(n_tp)]
        while len(terms) > 1:
            terms = [a + b for a, b in zip(terms[::2], terms[1::2])]
        for c in range(PACK // 2):
            first = half * (dout // 2) + c * chunk
            migrant_out[:, first : first + chunk] = terms[0][c : c + 1].astype(BF16)

    wait_sums(send_sem.at[6])


def first_served(n_inst):
    head = [7, 5, 1, 3]
    return head + [u for u in range(n_inst) if u not in head]


def far_first(n_inst):
    def hops(k):
        y, z = k // 8, k // 2 % 4
        return min(y, n_inst // 8 - y) + z

    return sorted(range(1, n_inst), key=lambda k: -hops(k))


def hand_over(resident, migrant, resident_out, migrant_out, sem):
    copies = [
        pltpu.make_async_copy(resident, resident_out, sem.at[0]),
        pltpu.make_async_copy(migrant, migrant_out, sem.at[1]),
    ]
    for c in copies:
        c.start()
    for c in copies:
        c.wait()


def on_device(n_inst, n_tp, *args):
    args = (*args[:5], args[5].T, args[6].T, *args[7:])
    key_cache, weight = args[1], args[11]
    rows, slots, _ = key_cache.shape
    dout = weight.shape[1]
    n_x = n_tp // 2
    block = (PACK, dout // n_x // 2)
    vmem = pltpu.VMEM
    dma = pltpu.SemaphoreType.DMA
    out_shape = (
        jax.ShapeDtypeStruct((rows, dout), BF16),
        jax.ShapeDtypeStruct((1, dout), BF16),
    )
    outs = pl.pallas_call(
        functools.partial(kernel, n_inst, n_tp),
        out_shape=out_shape,
        in_specs=[pl.BlockSpec(memory_space=pl.ANY)] * 12,
        out_specs=[pl.BlockSpec(memory_space=vmem)] * 2,
        scratch_shapes=[
            vmem((rows, GROUP * HEAD), BF16),
            vmem((rows, HEAD), BF16),
            vmem((rows, HEAD), BF16),
            vmem((1, GROUP * HEAD), BF16),
            vmem((1, HEAD), BF16),
            vmem((1, HEAD), BF16),
            vmem((rows, slots, HEAD), BF16),
            vmem((rows, slots, HEAD), BF16),
            vmem(weight.shape, BF16),
            pltpu.SMEM(args[5].shape, jnp.int32),
            pltpu.SMEM(args[6].shape, jnp.int32),
            pltpu.SMEM(args[7].shape, jnp.int32),
            vmem((rows, GROUP, HEAD), F32),
            vmem((n_inst, GROUP, HEAD), BF16),
            vmem((n_inst, 2, HEAD), BF16),
            vmem((n_inst, GROUP, HEAD), BF16),
            vmem((n_x, *block), BF16),
            vmem((n_x, *block), BF16),
            vmem((2, *block), BF16),
            vmem((n_x, *block), BF16),
            vmem((2 * n_tp, PACK // 2, dout // PACK), BF16),
            vmem((2, PACK // 2, dout // PACK), BF16),
            dma((9,)),
            dma,
            dma,
            dma,
            dma((7,)),
            dma((7,)),
        ],
        compiler_params=pltpu.CompilerParams(
            collective_id=0, has_side_effects=True, vmem_limit_bytes=48 * 1024 * 1024
        ),
    )(*[pltpu.with_memory_space_constraint(a, pltpu.HBM) for a in args])
    return pl.pallas_call(
        hand_over,
        out_shape=out_shape,
        in_specs=[pl.BlockSpec(memory_space=vmem)] * 2,
        out_specs=[pl.BlockSpec(memory_space=pl.ANY)] * 2,
        scratch_shapes=[dma((2,))],
        compiler_params=pltpu.CompilerParams(vmem_limit_bytes=4 * 1024 * 1024),
    )(*outs)


def solution(mesh):
    in_specs = (
        P("inst", "tp"),
        P("inst", None, "tp"),
        P("inst", None, "tp"),
        P("inst", "tp"),
        P("inst", "tp"),
        P(),
        P(),
        P(),
        P("inst", "tp"),
        P("inst", "tp"),
        P("inst", "tp"),
        P("tp", None),
    )
    out_specs = (P("inst", None), P("inst", None))
    return jax.shard_map(
        functools.partial(on_device, mesh.shape["inst"], mesh.shape["tp"]),
        mesh=mesh, in_specs=in_specs, out_specs=out_specs, check_vma=False,
    )
```
